32 devices in a mesh: dp: 16 (over z, y, core), tensor: 2 (over x).
Axes of the slice: x: 2, y: 2, z: 4, core: 2. Of those that a mesh axis runs over, the one named last changes fastest.
Arguments:
- inputs: bfloat16 [49152, 1024], P('dp'), may hold values from -6 to 6
- segment_ids: int32 [16, 3072], P('dp'), may hold values from 0 to 5, never falling along the last dimension, each value on 1 to 1024 neighbouring positions
- cotangent: bfloat16 [49152, 1024], P('dp', 'tensor'), may hold values from -6 to 6
- ln1_gain: bfloat16 [1024], replicated, may hold values from 0.5 to 1.5
- attention_norm_bias: bfloat16 [1024], replicated, may hold values from -3 to 3
- ln2_gain: bfloat16 [1024], replicated, may hold values from 0.5 to 1.5
- feedforward_norm_bias: bfloat16 [1024], replicated, may hold values from -3 to 3
- w_qkv: bfloat16 [1024, 3, 1024], P(None, None, 'tensor'), may hold values from -0.1875 to 0.1875
- b_qkv: bfloat16 [3, 1024], P(None, 'tensor'), may hold values from -3 to 3
- w_dense: bfloat16 [1024, 1024], P('tensor'), may hold values from -0.75 to 0.75
- b_dense: bfloat16 [1024], P('tensor'), may hold values from -3 to 3
- w_fc1: bfloat16 [1024, 4096], P(None, 'tensor'), may hold values from -0.1875 to 0.1875
- b_fc1: bfloat16 [4096], P('tensor'), may hold values from -3 to 3
- w_fc2: bfloat16 [4096, 1024], P('tensor'), may hold values from -0.09375 to 0.09375
- b_fc2: bfloat16 [1024], P('tensor'), may hold values from -3 to 3
Outputs:
- outputs: bfloat16 [49152, 1024], P('dp', 'tensor')
- input_grad: float32 [49152, 1024], P('dp', 'tensor')
- ln1_gain_grad: float32 [1024], replicated
- ln1_bias_grad: float32 [1024], replicated
- ln2_gain_grad: float32 [1024], replicated
- ln2_bias_grad: float32 [1024], replicated
- qkv_weight_grad: float32 [1024, 3, 1024], P(None, None, 'tensor')
- qkv_bias_grad: float32 [3, 1024], P(None, 'tensor')
- dense_weight_grad: float32 [1024, 1024], P('tensor')
- dense_bias_grad: float32 [1024], P('tensor')
- fc1_weight_grad: float32 [1024, 4096], P(None, 'tensor')
- fc1_bias_grad: float32 [4096], P('tensor')
- fc2_weight_grad: float32 [4096, 1024], P('tensor')
- fc2_bias_grad: float32 [1024], P('tensor')
The draws below stay inside these ranges and needn't reach their ends.
Inputs may be any that keep to these rules, and one draw needn't show every extreme that they name: `segment_ids`: in each pack of 3072 tokens the segment numbers never fall and run over 0 to 5; every segment has 1 to 1024 tokens, and one has exactly 1024.
All inputs are finite; a program needn't handle non-finite values.
Results may differ from the reference program's by a relative error of at most 0.012.
The reference program's roundings to bfloat16 on the way count: a program that leaves them out, or rounds other values in their place, can miss the bound.
Values may be sent and summed in bfloat16 or wider, within the bound.
No kernel may reach another device: no remote copies, remote signals or barrier semaphores. Data moves between devices by JAX's collectives and lax.ppermute only.
A program may use at most 320 MiB of HBM per device.

```python
import math
import jax
import jax.numpy as jnp
import numpy as np
from jax import lax

D = 1024
HEADS = 16
HEAD_DIM = 64
FF = 4096
ROT = 16
TOK_DEV = 3072
MOST = 1024
BLOCK = 512
SEQS = 6
ROWS = 16
TOKENS = 49152


def block_levels(own_key, dims, shards, smallest, largest):
    factor_of = 1.0
    for dim, shards_of in shards:
        draws = jax.random.uniform(jax.random.fold_in(jax.random.fold_in(own_key, 6), dim), (shards_of,), jnp.float32, smallest / len(shards), largest / len(shards))
        factor_of = factor_of * jnp.repeat(jnp.exp(draws), dims[dim] // shards_of).reshape((-1,) + (1,) * (len(dims) - 1 - dim))
    return factor_of


def length_profile(count, total, bound, slope):
    portions = [(1 << 20) // math.isqrt(standing ** slope) + 1 for standing in range(2, count + 1)]
    rest, holding = total - bound - (count - 1), [1] * (count - 1)
    while rest > 0:
        movable = [i for i in range(count - 1) if holding[i] < bound]
        pool, remaining = sum([portions[i] for i in movable]), rest
        for i in movable:
            extra = min(bound - holding[i], max(1, remaining * portions[i] // pool), rest)
            holding[i] = holding[i] + extra
            rest = rest - extra
    return np.array([bound] + holding)


def ragged_sizes(key, count, total, reach, slope):
    if count == 2:
        one = jax.random.randint(key, (), max(1, total - reach), min(reach, total - 1) + 1)
        return jnp.stack([one, total - one])
    tallies = jnp.asarray(length_profile(count, total, reach, slope), jnp.int32)
    pairs = (count - 1) // 2
    giver, receiver = tallies[1:1 + 2 * pairs:2], tallies[2:2 + 2 * pairs:2]
    room = jnp.minimum(giver - 1, reach - receiver)
    shifted = jax.random.randint(jax.random.fold_in(key, 1), (pairs,), 0, 1 << 20) % (room + 1)
    tallies = tallies.at[1:1 + 2 * pairs:2].set(giver - shifted).at[2:2 + 2 * pairs:2].set(receiver + shifted)
    return tallies[jax.random.permutation(jax.random.fold_in(key, 2), count)]


def noise(stream_key, dims, deviation, bound, cuts=(), held_as=jnp.bfloat16):
    array = jax.random.normal(stream_key, dims, jnp.float32) * deviation
    if len(cuts) > 0:
        array = block_levels(stream_key, dims, cuts, -0.22, 0.18) * array
    return jnp.clip(array, min=-bound, max=bound).astype(held_as)


def setup_inputs(seed: int = 0) -> dict:
    seeds = jax.random.split(jax.random.key(seed), 16)
    return {
        "inputs": noise(seeds[0], (TOKENS, D), 1.0, 6.0, ((0, 16),)),
        "segment_ids": jax.vmap(lambda own: jnp.searchsorted(jnp.cumsum(ragged_sizes(own, SEQS, TOK_DEV, MOST, 2)), jnp.arange(TOK_DEV), side="right"))(jax.random.split(seeds[1], ROWS)).reshape((ROWS, TOK_DEV)).astype(jnp.int32),
        "cotangent": noise(seeds[2], (TOKENS, D), 1.0, 6.0, ((0, 16), (1, 2))),
        "ln1_gain": jnp.clip(1.0 + 0.1 * jax.random.normal(seeds[3], (D,), jnp.float32), 0.5, 1.5).astype(jnp.bfloat16),
        "attention_norm_bias": noise(seeds[4], (D,), 0.5, 3.0),
        "ln2_gain": jnp.clip(1.0 + 0.1 * jax.random.normal(seeds[5], (D,), jnp.float32), 0.5, 1.5).astype(jnp.bfloat16),
        "feedforward_norm_bias": noise(seeds[6], (D,), 0.5, 3.0),
        "w_qkv": noise(seeds[7], (D, 3, D), D ** -0.5, 0.1875, ((2, 2),)),
        "b_qkv": noise(seeds[8], (3, D), 0.5, 3.0, ((1, 2),)),
        "w_dense": noise(seeds[9], (D, D), (max(D // 16, HEAD_DIM)) ** -0.5, 0.75, ((0, 2),)),
        "b_dense": noise(seeds[10], (D,), 0.5, 3.0, ((0, 2),)),
        "w_fc1": noise(seeds[11], (D, FF), D ** -0.5, 0.1875, ((1, 2),)),
        "b_fc1": noise(seeds[12], (FF,), 0.5, 3.0, ((0, 2),)),
        "w_fc2": noise(seeds[13], (FF, D), FF ** -0.5, 0.09375, ((0, 2),)),
        "b_fc2": noise(seeds[14], (D,), 0.5, 3.0, ((0, 2),)),
    }


@jax.custom_vjp
def low(v):
    return lax.optimization_barrier(v.astype(jnp.bfloat16)).astype(jnp.float32)

@jax.custom_vjp
def low_back(v):
    return v

def low_keep(v):
    return (low(v), None)

def low_pass(kept, grad):
    return (grad,)

def back_keep(v):
    return (v, None)

def back_low(kept, grad):
    return (low(grad),)
low.defvjp(low_keep, low_pass)
low_back.defvjp(back_keep, back_low)
NORM_EPS = 1e-05
MASKED = -1e+30
HIGHEST = lax.Precision.HIGHEST

def apply_layer_norm(values, gain, shift):
    centred = values - lax.optimization_barrier(jnp.mean(values, axis=-1, keepdims=True))
    root_inv = lax.rsqrt(lax.optimization_barrier(jnp.mean(centred * centred, axis=-1, keepdims=True)) + NORM_EPS)
    normed = centred * root_inv
    return (normed, root_inv, normed * gain + shift)

def rotary_tables(segments):
    length = segments.shape[0]
    places = jnp.arange(length, dtype=jnp.int32)
    first = jnp.concatenate([jnp.ones((1,), dtype=bool), segments[1:] != segments[:-1]])
    starts = lax.cummax(jnp.where(first, places, jnp.zeros_like(places)), axis=0)
    offsets = (places - starts).astype(jnp.float32)
    inverse = 10000.0 ** (-jnp.arange(0, ROT, 2).astype(jnp.float32) / ROT)
    angles = offsets[:, None] * inverse[None, :]
    cosine = jnp.concatenate([jnp.cos(angles), jnp.cos(angles)], axis=-1)
    sine = jnp.concatenate([jnp.sin(angles), jnp.sin(angles)], axis=-1)
    return (cosine, sine)

def rotate(values, cosine, sine):
    half = ROT // 2
    part = values[..., :ROT]
    turned = jnp.concatenate([-part[..., half:], part[..., :half]], axis=-1)
    moved = part * cosine[:, None, :] + turned * sine[:, None, :]
    return jnp.concatenate([moved, values[..., ROT:]], axis=-1)

def forward_pack(params, inputs, segments, cosine, sine):
    attention_norm_gain, shift_one, feedforward_norm_gain, shift_two, w_qkv, b_qkv, w_dense, b_dense, w_fc1, b_fc1, w_fc2, b_fc2 = params
    length = inputs.shape[0]
    scale = HEAD_DIM ** (-0.5)
    attention_normed = low(apply_layer_norm(inputs, attention_norm_gain, shift_one)[2])
    feedforward_normed = low(apply_layer_norm(inputs, feedforward_norm_gain, shift_two)[2])
    qkv = low_back(jnp.dot(attention_normed, w_qkv.reshape(D, 3 * D), precision=HIGHEST) + b_qkv.reshape(3 * D))
    qkv = qkv.reshape(length, 3, HEADS, HEAD_DIM)
    query = low(rotate(qkv[:, 0], cosine, sine))
    key = low(rotate(qkv[:, 1], cosine, sine))
    value = low(qkv[:, 2])
    places = jnp.arange(length, dtype=jnp.int32)

    def attend(start):
        rows_query = lax.dynamic_slice_in_dim(query, start, BLOCK, 0)
        seg_rows = lax.dynamic_slice_in_dim(segments, start, BLOCK, 0)
        pos_rows = lax.dynamic_slice_in_dim(places, start, BLOCK, 0)
        scores = low_back(scale * jnp.einsum('qhd,khd->hqk', rows_query, key, precision=HIGHEST))
        allowed = (seg_rows[:, None] == segments[None, :]) & (places[None, :] <= pos_rows[:, None])
        scores = jnp.where(allowed[None], scores, MASKED)
        log_total = jax.nn.logsumexp(scores, axis=-1, keepdims=True)
        probs = low(jnp.exp(scores - log_total))
        return jnp.einsum('hqk,khd->qhd', probs, value, precision=HIGHEST)
    starts = jnp.arange(length // BLOCK, dtype=jnp.int32) * BLOCK
    mixed = lax.map(jax.checkpoint(attend), starts).reshape(length, D)
    mixed = low_back(low(mixed))
    attention = jnp.dot(mixed, w_dense, precision=HIGHEST) + b_dense
    hidden = low_back(jnp.dot(feedforward_normed, w_fc1, precision=HIGHEST) + b_fc1)
    active = low(jax.nn.gelu(hidden, approximate=False))
    feed = jnp.dot(active, w_fc2, precision=HIGHEST) + b_fc2
    return inputs + attention + feed

def reference(inputs, segment_ids, cotangent, ln1_gain, attention_norm_bias, ln2_gain, feedforward_norm_bias, w_qkv, b_qkv, w_dense, b_dense, w_fc1, b_fc1, w_fc2, b_fc2):
    params = tuple((item.astype(jnp.float32) for item in (ln1_gain, attention_norm_bias, ln2_gain, feedforward_norm_bias, w_qkv, b_qkv, w_dense, b_dense, w_fc1, b_fc1, w_fc2, b_fc2)))
    packs = inputs.astype(jnp.float32).reshape(ROWS, TOK_DEV, D)
    grads_in = cotangent.astype(jnp.float32).reshape(ROWS, TOK_DEV, D)
    zeros = tuple((jnp.zeros_like(item) for item in params))

    def one_pack(total, pieces):
        rows_in, segments, rows_grad = pieces
        cosine, sine = rotary_tables(segments)
        result, pull = jax.vjp(lambda prm, val: forward_pack(prm, val, segments, cosine, sine), params, rows_in)
        param_grads, input_grad = pull(rows_grad)
        total = jax.tree.map(lambda left, right: left + right, total, param_grads)
        return (total, (result.astype(jnp.bfloat16), input_grad))
    total, (results, input_grads) = lax.scan(one_pack, zeros, (packs, segment_ids, grads_in))
    return (results.reshape(TOKENS, D), input_grads.reshape(TOKENS, D), total[0], total[1], total[2], total[3], total[4], total[5], total[6], total[7], total[8], total[9], total[10], total[11])
```

```python
import functools

import jax
import jax.numpy as jnp
from jax import lax
from jax.experimental import pallas as pl
from jax.experimental.pallas import tpu as pltpu
from jax.sharding import PartitionSpec as P

BQ = 256
BK = 256
PAIR = 128
NEG = -1e30
ROT = 16
NORM_EPS = 1e-05
VMEM = 60 * 1024 * 1024
GF = 4
GB = 4
AHEAD = 2
BEHIND = 2
AHEADB = 2
BEHINDB = 1
F32 = jnp.float32
BF = jnp.bfloat16
NT = (((1,), (1,)), ((), ()))
NN = (((1,), (0,)), ((), ()))
TN = (((0,), (0,)), ((), ()))

def mm(a, b, dims=NN):
    return lax.dot_general(a, b, dims, preferred_element_type=F32)

def lane_half(shape):
    return lax.broadcasted_iota(jnp.int32, shape, 1) < 64

def fwd_kernel(lo_ref, start_ref, q_ref, k_ref, v_ref, o_ref, lse_ref, vt_ref):
    length = q_ref.shape[0]
    nq = length // BQ
    nk = length // BK
    groups = q_ref.shape[1] // PAIR
    for i in range(nk):
        vt_ref[i] = jnp.transpose(v_ref[i * BK:(i + 1) * BK, :])
    first = lane_half((BQ, PAIR))

    def q_block(b, _):
        rows = pl.ds(pl.multiple_of(b * BQ, BQ), BQ)
        qs = []
        for g in range(groups):
            q = q_ref[rows, PAIR * g:PAIR * g + PAIR]
            zero = jnp.zeros_like(q)
            qs += [jnp.where(first, q, zero), jnp.where(first, zero, q)]
        starts = start_ref[pl.ds(b, 1), :]
        def step(kb, carry, diagonal):
            keys = pl.ds(pl.multiple_of(kb * BK, BK), BK)
            place = lax.broadcasted_iota(jnp.int32, (BK, BQ), 0)
            allowed = place >= starts - kb * BK
            if diagonal:
                allowed = allowed & (place <= lax.broadcasted_iota(jnp.int32, (BK, BQ), 1))
            heads = range(2 * groups)
            scores, weights, out = {}, {}, []
            def score(h):
                if h in heads:
                    k = k_ref[keys, PAIR * (h // 2):PAIR * (h // 2) + PAIR]
                    scores[h] = mm(k, qs[h], NT)
            def soften(h):
                m, l, acc = carry[h]
                s = jnp.where(allowed, scores[h], NEG)
                m_new = jnp.maximum(m, jnp.max(s, axis=0, keepdims=True))
                p = jnp.exp(s - m_new)
                alpha = jnp.exp(m - m_new)
                weights[h] = (m_new, l * alpha + jnp.sum(p, axis=0, keepdims=True), alpha, p.astype(BF))
            def mix(h):
                m_new, l, alpha, p = weights[h]
                out.append((m_new, l, carry[h][2] * alpha + mm(vt_ref[kb, 64 * h:64 * h + 64, :], p)))
            for h in range(AHEAD):
                score(h)
            for h in heads:
                score(h + AHEAD)
                soften(h)
                if h >= BEHIND:
                    mix(h - BEHIND)
            for h in heads[len(heads) - BEHIND:] if BEHIND else ():
                mix(h)
            return tuple(out)
        init = tuple((jnp.full((1, BQ), NEG, F32), jnp.zeros((1, BQ), F32), jnp.zeros((64, BQ), F32)) for _ in range(2 * groups))
        carry = step(b, init, True)
        carry = lax.fori_loop(lo_ref[b], b, lambda kb, c: step(kb, c, False), carry)
        for h in range(2 * groups):
            lse_ref[h, pl.ds(b, 1), :] = carry[h][0] + jnp.log(carry[h][1])
        ot = jnp.concatenate([c[2] / c[1] for c in carry], axis=0)
        o_ref[rows, :] = jnp.transpose(ot).astype(BF)
        return 0
    lax.fori_loop(0, nq, q_block, 0)

def attn_fwd(lo, starts, q, k, v):
    length, width = q.shape
    nq = length // BQ
    group = min(GF * PAIR, width)
    pairs = width // group
    col = pl.BlockSpec((length, group), lambda p, *_: (0, p))
    return pl.pallas_call(
        fwd_kernel,
        grid_spec=pltpu.PrefetchScalarGridSpec(
            num_scalar_prefetch=1, grid=(pairs,),
            in_specs=[pl.BlockSpec((nq, BQ), lambda p, *_: (0, 0)), col, col, col],
            out_specs=[col, pl.BlockSpec((group // 64, nq, BQ), lambda p, *_: (p, 0, 0))],
            scratch_shapes=[pltpu.VMEM((length // BK, group, BK), BF)],
        ),
        out_shape=[jax.ShapeDtypeStruct((length, width), BF), jax.ShapeDtypeStruct((width // 64, nq, BQ), F32)],
        compiler_params=pltpu.CompilerParams(vmem_limit_bytes=VMEM),
        name="attention_forward",
    )(lo, starts, q, k, v)

def bwd_kernel(lo_ref, start_ref, q_ref, k_ref, v_ref, o_ref, do_ref, lse_ref, cos_ref, sa_ref, sb_ref, dq_ref, dk_ref, dv_ref, kt_ref, dk_acc, dv_acc):
    length = q_ref.shape[0]
    nq = length // BQ
    nk = length // BK
    groups = q_ref.shape[1] // PAIR
    for i in range(nk):
        kt_ref[i] = jnp.transpose(k_ref[i * BK:(i + 1) * BK, :])
    first = lane_half((BQ, PAIR))
    dk_acc[...] = jnp.zeros_like(dk_acc)
    dv_acc[...] = jnp.zeros_like(dv_acc)

    def unrotate(w, rows):
        return w * cos_ref[rows, :] - pltpu.roll(w, PAIR - 8, 1) * sa_ref[rows, :] - pltpu.roll(w, 8, 1) * sb_ref[rows, :]

    cols = [slice(PAIR * g, PAIR * g + PAIR) for g in range(groups)]

    def q_block(step_index, _):
        b = nq - 1 - step_index
        rows = pl.ds(pl.multiple_of(b * BQ, BQ), BQ)
        starts = start_ref[pl.ds(b, 1), :]
        qs, dos, deltas, lses = [], [], [], []
        for g in range(groups):
            q = q_ref[rows, cols[g]]
            do = do_ref[rows, cols[g]]
            zero = jnp.zeros_like(q)
            qs += [jnp.where(first, q, zero), jnp.where(first, zero, q)]
            dos += [jnp.where(first, do, zero), jnp.where(first, zero, do)]
            prod = jnp.transpose(do.astype(F32) * o_ref[rows, cols[g]].astype(F32))
            deltas += [jnp.sum(prod[:64], axis=0, keepdims=True), jnp.sum(prod[64:], axis=0, keepdims=True)]
            lses += [lse_ref[2 * g, pl.ds(b, 1), :], lse_ref[2 * g + 1, pl.ds(b, 1), :]]
        def step(kb, carry, diagonal):
            keys = pl.ds(pl.multiple_of(kb * BK, BK), BK)
            place = lax.broadcasted_iota(jnp.int32, (BK, BQ), 0)
            allowed = place >= starts - kb * BK
            if diagonal:
                allowed = allowed & (place <= lax.broadcasted_iota(jnp.int32, (BK, BQ), 1))
            out = []
            heads = range(2 * groups)
            raw, soft = {}, {}
            def score(h):
                if h in heads:
                    raw[h] = (mm(k_ref[keys, cols[h // 2]], qs[h], NT), mm(v_ref[keys, cols[h // 2]], dos[h], NT))
            def soften(h):
                s, dp = raw[h]
                p = jnp.exp(jnp.where(allowed, s - lses[h], NEG))
                soft[h] = (p.astype(BF), (p * (dp - deltas[h])).astype(BF))
            def mix(h):
                out.append(carry[h] + mm(kt_ref[kb, 64 * h:64 * h + 64, :], soft[h][1]))
                if h % 2 == 1:
                    g = h // 2
                    dv_acc[keys, cols[g]] += mm(jnp.concatenate([soft[h - 1][0], soft[h][0]], axis=1), jnp.concatenate(dos[2 * g:2 * g + 2], axis=0))
                    dk_acc[keys, cols[g]] += mm(jnp.concatenate([soft[h - 1][1], soft[h][1]], axis=1), jnp.concatenate(qs[2 * g:2 * g + 2], axis=0))
            for h in range(AHEADB):
                score(h)
            for h in heads:
                score(h + AHEADB)
                soften(h)
                if h >= BEHINDB:
                    mix(h - BEHINDB)
            for h in heads[len(heads) - BEHINDB:] if BEHINDB else ():
                mix(h)
            return tuple(out)
        carry = tuple(jnp.zeros((64, BQ), F32) for _ in range(2 * groups))
        carry = lax.fori_loop(lo_ref[b], b, lambda kb, c: step(kb, c, False), carry)
        carry = step(b, carry, True)
        for g in range(groups):
            dq = jnp.transpose(jnp.concatenate(carry[2 * g:2 * g + 2], axis=0)) * 0.125
            dq_ref[rows, cols[g]] = unrotate(dq, rows).astype(BF)
            dk_ref[rows, cols[g]] = unrotate(dk_acc[rows, cols[g]], rows).astype(BF)
            dv_ref[rows, cols[g]] = dv_acc[rows, cols[g]].astype(BF)
        return 0
    lax.fori_loop(0, nq, q_block, 0)

def attn_bwd(lo, starts, q, k, v, o, do, lse, cos, sa, sb):
    length, width = q.shape
    nq = length // BQ
    group = min(GB * PAIR, width)
    pairs = width // group
    col = pl.BlockSpec((length, group), lambda p, *_: (0, p))
    whole = pl.BlockSpec((length, PAIR), lambda p, *_: (0, 0))
    return pl.pallas_call(
        bwd_kernel,
        grid_spec=pltpu.PrefetchScalarGridSpec(
            num_scalar_prefetch=1, grid=(pairs,),
            in_specs=[pl.BlockSpec((nq, BQ), lambda p, *_: (0, 0)), col, col, col, col, col,
                      pl.BlockSpec((group // 64, nq, BQ), lambda p, *_: (p, 0, 0)), whole, whole, whole],
            out_specs=[col, col, col],
            scratch_shapes=[pltpu.VMEM((length // BK, group, BK), BF), pltpu.VMEM((length, group), F32), pltpu.VMEM((length, group), F32)],
        ),
        out_shape=[jax.ShapeDtypeStruct((length, width), BF)] * 3,
        compiler_params=pltpu.CompilerParams(vmem_limit_bytes=VMEM),
        name="attention_backward",
    )(lo, starts, q, k, v, o, do, lse, cos, sa, sb)

T = 512
TT = 512


def norm_rows(x, eps=NORM_EPS):
    centred = x - jnp.mean(x, axis=-1, keepdims=True)
    root_inv = lax.rsqrt(jnp.mean(centred * centred, axis=-1, keepdims=True) + eps)
    return centred * root_inv, root_inv


def fold_rows(v):
    return jnp.sum(v.reshape(v.shape[0] // 8, 8, v.shape[1]), axis=0)


def project_kernel(x_ref, gain_ref, shift_ref, w_ref, b_ref, cos_ref, sa_ref, sb_ref, q_ref, k_ref, v_ref):
    local = q_ref.shape[1]
    xhat, _ = norm_rows(x_ref[...].astype(F32))
    normed = (xhat * gain_ref[...] + shift_ref[...]).astype(BF)
    for which, out in enumerate((q_ref, k_ref, v_ref)):
        span = slice(which * local, which * local + local)
        y = mm(normed, w_ref[:, span]) + b_ref[:, span]
        if which == 2:
            out[...] = y.astype(BF)
            continue
        for c in range(local // PAIR):
            cols = slice(c * PAIR, c * PAIR + PAIR)
            u = y[:, cols]
            u = u * cos_ref[...] + pltpu.roll(u, PAIR - 8, 1) * sa_ref[...] + pltpu.roll(u, 8, 1) * sb_ref[...]
            out[:, cols] = (u * 0.125 if which == 0 else u).astype(BF)


def fixed(shape):
    return pl.BlockSpec(shape, lambda i, *_: (0,) * len(shape), pipeline_mode=pl.Buffered(1))


def tokens(rows, cols):
    return pl.BlockSpec((rows, cols), lambda i, *_: (i, 0))


def project(x, gain, shift, w, b, cos, sa, sb):
    length, width = x.shape
    local = w.shape[1] // 3
    return pl.pallas_call(
        project_kernel,
        grid=(length // T,),
        in_specs=[tokens(T, width), fixed((1, width)), fixed((1, width)), fixed(w.shape), fixed(b.shape)] + [tokens(T, PAIR)] * 3,
        out_specs=[tokens(T, local)] * 3,
        out_shape=[jax.ShapeDtypeStruct((length, local), BF)] * 3,
        compiler_params=pltpu.CompilerParams(vmem_limit_bytes=VMEM),
        cost_estimate=pl.CostEstimate(flops=2 * length * width * 3 * local, bytes_accessed=length * width * 4, transcendentals=0),
        name="project_qkv",
    )(x, gain, shift, w, b, cos, sa, sb)


def scatter_pieces(total, me, outs):
    ranks, local = len(outs), outs[0].shape[1]
    for d in range(ranks):
        target = lax.rem(me + d, ranks)
        cols = pl.ds(pl.multiple_of(target * local, 128), local)
        outs[d][...] = total[:, cols].astype(outs[d].dtype)


def feedforward_kernel(ranks, me_ref, x_ref, gain_ref, shift_ref, w1_ref, b1_ref, w2_ref, wd_ref, mixed_ref, *refs):
    pieces, refs = refs[:ranks], refs[ranks:]
    outs, refs = refs[:ranks], refs[ranks:]
    mixed_grad_ref, n2g_ref, w1g_ref, w2g_ref, wdg_ref, b1g_ref, lng_ref, lnb_ref, g_ref, n2t_ref, total_ref, back_ref = refs
    step = pl.program_id(0)
    me = me_ref[0]
    local = pieces[0].shape[1]
    hidden_units = w1_ref.shape[1]
    chunk = min(512, hidden_units)
    chunks = hidden_units // chunk

    @pl.when(step == 0)
    def _():
        for ref in (w1g_ref, w2g_ref, wdg_ref, b1g_ref, lng_ref, lnb_ref):
            ref[...] = jnp.zeros_like(ref)

    for d in range(ranks):
        source = lax.rem(me + d, ranks)
        g_ref[:, pl.ds(pl.multiple_of(source * local, 128), local)] = pieces[d][...]
    xhat, _ = norm_rows(x_ref[...].astype(F32))
    normed = (xhat * gain_ref[...] + shift_ref[...]).astype(BF)
    n2t_ref[...] = jnp.transpose(normed)
    g = g_ref[...]
    raw, soft = {}, {}

    def expand(c):
        if c < chunks:
            cols = slice(c * chunk, c * chunk + chunk)
            raw[c] = (mm(normed, w1_ref[:, cols]) + b1_ref[:, cols], mm(g, w2_ref[cols, :], NT))

    def bend(c):
        cols = slice(c * chunk, c * chunk + chunk)
        hidden, active_grad = raw[c]
        cumulative = 0.5 * (1.0 + lax.erf(hidden * 0.7071067811865476))
        density = jnp.exp(-0.5 * hidden * hidden) * 0.3989422804014327
        active = (hidden * cumulative).astype(BF)
        hidden_grad = (active_grad * (cumulative + hidden * density)).astype(BF)
        b1g_ref[:, cols] += fold_rows(hidden_grad.astype(F32))
        soft[c] = (active, hidden_grad)

    def contract(c):
        cols = slice(c * chunk, c * chunk + chunk)
        active, hidden_grad = soft[c]
        feed = mm(active, w2_ref[cols, :])
        back = mm(hidden_grad, w1_ref[:, cols], NT)
        if c == 0:
            total_ref[...] = feed
            back_ref[...] = back
        else:
            total_ref[...] += feed
            back_ref[...] += back
        w2g_ref[cols, :] += mm(active, g, TN)
        w1g_ref[:, cols] += mm(n2t_ref[...], hidden_grad)

    expand(0)
    for c in range(chunks):
        expand(c + 1)
        bend(c)
        if c >= 1:
            contract(c - 1)
    mixed = mixed_ref[...]
    mixed_grad_ref[...] = mm(g, wd_ref[...], NT).astype(BF)
    contract(chunks - 1)
    total_ref[...] += mm(mixed, wd_ref[...])
    wdg_ref[...] += mm(mixed, g, TN)
    back = back_ref[...]
    n2g_ref[...] = back.astype(BF)
    lnb_ref[...] += fold_rows(back)
    lng_ref[...] += fold_rows(back * xhat)
    scatter_pieces(total_ref, me, outs)


def feedforward(me, x, gain, shift, w1, b1, w2, wd, mixed, pieces):
    length, width = x.shape
    local, hidden_units, ranks = mixed.shape[1], w1.shape[1], len(pieces)
    shapes = [((length, local), F32)] + [((length, local), BF)] * (ranks - 1) + [((length, local), BF), ((length, width), BF)]
    sums = [(width, hidden_units), (hidden_units, width), (local, width), (8, hidden_units), (8, width), (8, width)]
    return pl.pallas_call(
        functools.partial(feedforward_kernel, ranks),
        grid_spec=pltpu.PrefetchScalarGridSpec(
            num_scalar_prefetch=1,
            grid=(length // TT,),
            in_specs=[tokens(TT, width), fixed((1, width)), fixed((1, width)), fixed(w1.shape), fixed(b1.shape), fixed(w2.shape), fixed(wd.shape), tokens(TT, local)]
            + [tokens(TT, local)] * ranks,
            out_specs=[tokens(TT, s[1]) for s, _ in shapes] + [fixed(s) for s in sums],
            scratch_shapes=[pltpu.VMEM((TT, width), BF), pltpu.VMEM((width, TT), BF), pltpu.VMEM((TT, width), F32), pltpu.VMEM((TT, width), F32)],
        ),
        out_shape=[jax.ShapeDtypeStruct(s, d) for s, d in shapes] + [jax.ShapeDtypeStruct(s, F32) for s in sums],
        compiler_params=pltpu.CompilerParams(vmem_limit_bytes=VMEM),
        cost_estimate=pl.CostEstimate(flops=2 * length * width * (6 * hidden_units + 3 * local), bytes_accessed=length * width * 12, transcendentals=length * hidden_units),
        name="feedforward_both_ways",
    )(me, x, gain, shift, w1, b1, w2, wd, mixed, *pieces)


def input_kernel(ranks, me_ref, x_ref, gain1_ref, shift1_ref, gain2_ref, w_ref, dq_ref, dk_ref, dv_ref, n2g_ref, *refs):
    outs, refs = refs[:ranks], refs[ranks:]
    wg_ref, bg_ref, lng_ref, lnb_ref, n1t_ref, total_ref = refs
    local = dq_ref.shape[1]

    @pl.when(pl.program_id(0) == 0)
    def _():
        for ref in (wg_ref, bg_ref, lng_ref, lnb_ref):
            ref[...] = jnp.zeros_like(ref)

    xhat, root_inv = norm_rows(x_ref[...].astype(F32))
    n1t_ref[...] = jnp.transpose((xhat * gain1_ref[...] + shift1_ref[...]).astype(BF))
    grads = (dq_ref[...], dk_ref[...], dv_ref[...])
    spans = [slice(w * local, w * local + local) for w in range(3)]
    back = mm(grads[0], w_ref[:, spans[0]], NT) + mm(grads[1], w_ref[:, spans[1]], NT) + mm(grads[2], w_ref[:, spans[2]], NT)
    for grad, span in zip(grads, spans):
        wg_ref[:, span] += mm(n1t_ref[...], grad)
        bg_ref[:, span] += fold_rows(grad.astype(F32))
    lnb_ref[...] += fold_rows(back)
    lng_ref[...] += fold_rows(back * xhat)
    e = back * gain1_ref[...] + n2g_ref[...].astype(F32) * gain2_ref[...]
    total_ref[...] = root_inv * (e - jnp.mean(e, axis=-1, keepdims=True) - xhat * jnp.mean(e * xhat, axis=-1, keepdims=True))
    scatter_pieces(total_ref, me_ref[0], outs)


def input_backward(me, ranks, x, gain1, shift1, gain2, w, dq, dk, dv, n2g):
    length, width = x.shape
    local = dq.shape[1]
    shapes = [((length, local), F32)] + [((length, local), BF)] * (ranks - 1)
    sums = [w.shape, (8, w.shape[1]), (8, width), (8, width)]
    return pl.pallas_call(
        functools.partial(input_kernel, ranks),
        grid_spec=pltpu.PrefetchScalarGridSpec(
            num_scalar_prefetch=1,
            grid=(length // T,),
            in_specs=[tokens(T, width), fixed((1, width)), fixed((1, width)), fixed((1, width)), fixed(w.shape)] + [tokens(T, local)] * 3 + [tokens(T, width)],
            out_specs=[tokens(T, s[1]) for s, _ in shapes] + [fixed(s) for s in sums],
            scratch_shapes=[pltpu.VMEM((width, T), BF), pltpu.VMEM((T, width), F32)],
        ),
        out_shape=[jax.ShapeDtypeStruct(s, d) for s, d in shapes] + [jax.ShapeDtypeStruct(s, F32) for s in sums],
        compiler_params=pltpu.CompilerParams(vmem_limit_bytes=VMEM),
        cost_estimate=pl.CostEstimate(flops=2 * length * width * 6 * local, bytes_accessed=length * width * 12, transcendentals=0),
        name="input_backward",
    )(me, x, gain1, shift1, gain2, w, dq, dk, dv, n2g)


def sum_weights(grads, packs):
    return [v.astype(F32) for v in lax.psum(tuple(v.astype(BF) for v in grads), "dp")]


def rotary_tables(segments):
    length = segments.shape[0]
    places = jnp.arange(length, dtype=jnp.int32)
    first = jnp.concatenate([jnp.ones((1,), dtype=bool), segments[1:] != segments[:-1]])
    starts = lax.cummax(jnp.where(first, places, jnp.zeros_like(places)), axis=0)
    offsets = (places - starts).astype(F32)
    lane = jnp.arange(PAIR, dtype=jnp.int32) % 64
    inverse = 10000.0 ** (-(2 * (lane % (ROT // 2))).astype(F32) / ROT)
    angles = offsets[:, None] * inverse[None, :]
    cosine, sine = jnp.cos(angles), jnp.sin(angles)
    turned = lane < ROT
    low = lane < ROT // 2
    return (
        starts,
        jnp.where(turned, cosine, 1.0),
        jnp.where(low, -sine, 0.0),
        jnp.where(turned & ~low, sine, 0.0),
    )


def shifted(ranks, distance):
    return [(i, (i + distance) % ranks) for i in range(ranks)]


def send_pieces(pieces):
    ranks = len(pieces)
    total = pieces[0]
    for d in range(1, ranks):
        total = total + lax.ppermute(pieces[d], "tensor", shifted(ranks, d)).astype(F32)
    return total


def swap_sum(value, axis, ranks):
    step = 1
    while step < ranks:
        value = value + lax.ppermute(value, axis, [(i, i ^ step) for i in range(ranks)])
        step *= 2
    return value


def on_device(sizes, inputs, segment_ids, cotangent, ln1_gain, attention_norm_bias, ln2_gain, feedforward_norm_bias, w_qkv, b_qkv, w_dense, b_dense, w_fc1, b_fc1, w_fc2, b_fc2):
    packs, ranks = sizes
    segments = segment_ids[0]
    width = inputs.shape[1]
    local = w_qkv.shape[2]
    hidden_units = w_fc1.shape[1]
    me = lax.axis_index("tensor").astype(jnp.int32).reshape(1)
    pieces = [cotangent] + [lax.ppermute(cotangent, "tensor", shifted(ranks, ranks - d)) for d in range(1, ranks)]
    starts, cosine, sine_a, sine_b = rotary_tables(segments)
    starts = starts.reshape(-1, BQ)
    lowest = starts[:, 0] // BK
    row = lambda v: v.astype(F32).reshape(1, -1)
    qkv_matrix = w_qkv.reshape(width, 3 * local)
    gain1, gain2 = row(ln1_gain), row(ln2_gain)
    shift1, shift2 = row(attention_norm_bias), row(feedforward_norm_bias)
    query, key, value = project(inputs, gain1, shift1, qkv_matrix, row(b_qkv), cosine, sine_a, sine_b)
    mixed, totals = attn_fwd(lowest, starts, query, key, value)
    made = feedforward(me, inputs, gain2, shift2, w_fc1, row(b_fc1), w_fc2, w_dense, mixed, pieces)
    outs, (mixed_grad, normed2_grad, w1g, w2g, wdg, b1g, ln2g, ln2b) = made[:ranks], made[ranks:]
    own = lax.dynamic_slice_in_dim(inputs, me[0] * local, local, 1).astype(F32)
    outputs = (send_pieces(outs) + own + b_dense.astype(F32) + b_fc2.astype(F32)).astype(BF)
    big = sum_weights((w1g, w2g, wdg), packs)
    dq, dk, dv = attn_bwd(lowest, starts, query, key, value, mixed, mixed_grad, totals, cosine, sine_a, sine_b)
    made = input_backward(me, ranks, inputs, gain1, shift1, gain2, qkv_matrix, dq, dk, dv, normed2_grad)
    partials, (wg, bg, ln1g, ln1b) = made[:ranks], made[ranks:]
    input_grad = send_pieces(partials) + cotangent.astype(F32)
    (wg,) = sum_weights((wg,), packs)
    out_bias = jnp.sum(cotangent.astype(F32), axis=0)
    norms = jnp.stack([jnp.sum(v, axis=0) for v in (ln1g, ln1b, ln2g, ln2b)]).reshape(-1)
    norms = swap_sum(norms, "tensor", ranks)
    biases = (jnp.sum(bg, axis=0), out_bias, jnp.sum(b1g, axis=0))
    small = jnp.concatenate((norms,) + biases).reshape(-1, 128)
    small = swap_sum(small, "dp", packs).reshape(-1)
    norms = small[: 4 * width].reshape(4, width)
    small = small[4 * width :]
    qkv_bias_grad = small[: 3 * local].reshape(3, local)
    dense_bias_grad = small[3 * local : 4 * local]
    fc1_bias_grad = small[4 * local :]
    return (
        outputs,
        input_grad,
        norms[0],
        norms[1],
        norms[2],
        norms[3],
        wg.reshape(width, 3, local),
        qkv_bias_grad,
        big[2],
        dense_bias_grad,
        big[0],
        fc1_bias_grad,
        big[1],
        dense_bias_grad,
    )


def solution(mesh):
    placed = (
        P("dp", None),
        P("dp", None),
        P("dp", "tensor"),
        P(),
        P(),
        P(),
        P(),
        P(None, None, "tensor"),
        P(None, "tensor"),
        P("tensor", None),
        P("tensor"),
        P(None, "tensor"),
        P("tensor"),
        P("tensor", None),
        P("tensor"),
    )
    sizes = (mesh.shape["dp"], mesh.shape["tensor"])
    return jax.shard_map(
        functools.partial(on_device, sizes),
        mesh=mesh,
        in_specs=placed,
        out_specs=(
            P("dp", "tensor"),
            P("dp", "tensor"),
            P(),
            P(),
            P(),
            P(),
            P(None, None, "tensor"),
            P(None, "tensor"),
            P("tensor", None),
            P("tensor"),
            P(None, "tensor"),
            P("tensor"),
            P("tensor", None),
            P("tensor"),
        ),
        check_vma=False,
    )
```

```python
import functools

import jax
import jax.numpy as jnp
from jax import lax
from jax.experimental import pallas as pl
from jax.experimental.pallas import tpu as pltpu
from jax.sharding import PartitionSpec as P

BQ = 256
BK = 256
PAIR = 128
NEG = -1e30
ROT = 16
NORM_EPS = 1e-05
VMEM = 60 * 1024 * 1024
COST = pl.CostEstimate(flops=1, bytes_accessed=1, transcendentals=0)
GF = 4
GB = 4
AHEAD = 2
BEHIND = 2
AHEADB = 2
BEHINDB = 1
F32 = jnp.float32
BF = jnp.bfloat16
NT = (((1,), (1,)), ((), ()))
NN = (((1,), (0,)), ((), ()))
TN = (((0,), (0,)), ((), ()))

def mm(a, b, dims=NN):
    return lax.dot_general(a, b, dims, preferred_element_type=F32)

def rotary_lanes(cos, sin):
    rest = jnp.ones((64 - ROT, cos.shape[1]), F32)
    none = jnp.zeros((64 - ROT, cos.shape[1]), F32)
    blank = jnp.zeros_like(cos)
    wide = jnp.concatenate([cos, cos, rest] * 2, axis=0)
    low = jnp.concatenate([-sin, blank, none] * 2, axis=0)
    high = jnp.concatenate([blank, sin, none] * 2, axis=0)
    return jnp.transpose(wide), jnp.transpose(low), jnp.transpose(high)


def lane_half(shape):
    return lax.broadcasted_iota(jnp.int32, shape, 1) < 64

def fwd_kernel(lo_ref, start_ref, q_ref, k_ref, v_ref, o_ref, lse_ref, vt_ref):
    length = q_ref.shape[0]
    nq = length // BQ
    nk = length // BK
    groups = q_ref.shape[1] // PAIR
    for i in range(nk):
        vt_ref[i] = jnp.transpose(v_ref[i * BK:(i + 1) * BK, :])
    first = lane_half((BQ, PAIR))

    def q_block(b, _):
        rows = pl.ds(pl.multiple_of(b * BQ, BQ), BQ)
        qs = []
        for g in range(groups):
            q = q_ref[rows, PAIR * g:PAIR * g + PAIR]
            zero = jnp.zeros_like(q)
            qs += [jnp.where(first, q, zero), jnp.where(first, zero, q)]
        starts = start_ref[pl.ds(b, 1), :]
        def step(kb, carry, diagonal):
            keys = pl.ds(pl.multiple_of(kb * BK, BK), BK)
            place = lax.broadcasted_iota(jnp.int32, (BK, BQ), 0)
            allowed = place >= starts - kb * BK
            if diagonal:
                allowed = allowed & (place <= lax.broadcasted_iota(jnp.int32, (BK, BQ), 1))
            heads = range(2 * groups)
            scores, weights, out = {}, {}, []
            def score(h):
                if h in heads:
                    k = k_ref[keys, PAIR * (h // 2):PAIR * (h // 2) + PAIR]
                    scores[h] = mm(k, qs[h], NT)
            def soften(h):
                m, l, acc = carry[h]
                s = jnp.where(allowed, scores[h], NEG)
                m_new = jnp.maximum(m, jnp.max(s, axis=0, keepdims=True))
                p = jnp.exp(s - m_new)
                alpha = jnp.exp(m - m_new)
                weights[h] = (m_new, l * alpha + jnp.sum(p, axis=0, keepdims=True), alpha, p.astype(BF))
            def mix(h):
                m_new, l, alpha, p = weights[h]
                out.append((m_new, l, carry[h][2] * alpha + mm(vt_ref[kb, 64 * h:64 * h + 64, :], p)))
            for h in range(AHEAD):
                score(h)
            for h in heads:
                score(h + AHEAD)
                soften(h)
                if h >= BEHIND:
                    mix(h - BEHIND)
            for h in heads[len(heads) - BEHIND:] if BEHIND else ():
                mix(h)
            return tuple(out)
        init = tuple((jnp.full((1, BQ), NEG, F32), jnp.zeros((1, BQ), F32), jnp.zeros((64, BQ), F32)) for _ in range(2 * groups))
        carry = step(b, init, True)
        carry = lax.fori_loop(lo_ref[b], b, lambda kb, c: step(kb, c, False), carry)
        for h in range(2 * groups):
            lse_ref[h, pl.ds(b, 1), :] = carry[h][0] + jnp.log(carry[h][1])
        ot = jnp.concatenate([c[2] / c[1] for c in carry], axis=0)
        o_ref[rows, :] = jnp.transpose(ot).astype(BF)
        return 0
    lax.fori_loop(0, nq, q_block, 0)

def attn_fwd(lo, starts, q, k, v):
    length, width = q.shape
    nq = length // BQ
    group = min(GF * PAIR, width)
    pairs = width // group
    col = pl.BlockSpec((length, group), lambda p, *_: (0, p))
    return pl.pallas_call(
        fwd_kernel,
        grid_spec=pltpu.PrefetchScalarGridSpec(
            num_scalar_prefetch=1, grid=(pairs,),
            in_specs=[pl.BlockSpec((nq, BQ), lambda p, *_: (0, 0)), col, col, col],
            out_specs=[col, pl.BlockSpec((group // 64, nq, BQ), lambda p, *_: (p, 0, 0))],
            scratch_shapes=[pltpu.VMEM((length // BK, group, BK), BF)],
        ),
        out_shape=[jax.ShapeDtypeStruct((length, width), BF), jax.ShapeDtypeStruct((width // 64, nq, BQ), F32)],
        compiler_params=pltpu.CompilerParams(vmem_limit_bytes=VMEM),
        cost_estimate=COST,
        name="attention_forward",
    )(lo, starts, q, k, v)

def bwd_kernel(lo_ref, start_ref, q_ref, k_ref, v_ref, o_ref, do_ref, lse_ref, cos_ref, sin_ref, dq_ref, dk_ref, dv_ref, kt_ref, dk_acc, dv_acc):
    length = q_ref.shape[0]
    nq = length // BQ
    nk = length // BK
    groups = q_ref.shape[1] // PAIR
    for i in range(nk):
        kt_ref[i] = jnp.transpose(k_ref[i * BK:(i + 1) * BK, :])
    first = lane_half((BQ, PAIR))
    dk_acc[...] = jnp.zeros_like(dk_acc)
    dv_acc[...] = jnp.zeros_like(dv_acc)

    cols = [slice(PAIR * g, PAIR * g + PAIR) for g in range(groups)]

    def q_block(step_index, _):
        b = nq - 1 - step_index
        rows = pl.ds(pl.multiple_of(b * BQ, BQ), BQ)
        starts = start_ref[pl.ds(b, 1), :]
        qs, dos, deltas, lses = [], [], [], []
        for g in range(groups):
            q = q_ref[rows, cols[g]]
            do = do_ref[rows, cols[g]]
            zero = jnp.zeros_like(q)
            qs += [jnp.where(first, q, zero), jnp.where(first, zero, q)]
            dos += [jnp.where(first, do, zero), jnp.where(first, zero, do)]
            prod = jnp.transpose(do.astype(F32) * o_ref[rows, cols[g]].astype(F32))
            deltas += [jnp.sum(prod[:64], axis=0, keepdims=True), jnp.sum(prod[64:], axis=0, keepdims=True)]
            lses += [lse_ref[2 * g, pl.ds(b, 1), :], lse_ref[2 * g + 1, pl.ds(b, 1), :]]
        def step(kb, carry, diagonal):
            keys = pl.ds(pl.multiple_of(kb * BK, BK), BK)
            place = lax.broadcasted_iota(jnp.int32, (BK, BQ), 0)
            allowed = place >= starts - kb * BK
            if diagonal:
                allowed = allowed & (place <= lax.broadcasted_iota(jnp.int32, (BK, BQ), 1))
            out = []
            heads = range(2 * groups)
            raw, soft = {}, {}
            def score(h):
                if h in heads:
                    raw[h] = (mm(k_ref[keys, cols[h // 2]], qs[h], NT), mm(v_ref[keys, cols[h // 2]], dos[h], NT))
            def soften(h):
                s, dp = raw[h]
                p = jnp.exp(jnp.where(allowed, s - lses[h], NEG))
                soft[h] = (p.astype(BF), (p * (dp - deltas[h])).astype(BF))
            def mix(h):
                out.append(carry[h] + mm(kt_ref[kb, 64 * h:64 * h + 64, :], soft[h][1]))
                if h % 2 == 1:
                    g = h // 2
                    dv_acc[keys, cols[g]] += mm(jnp.concatenate([soft[h - 1][0], soft[h][0]], axis=1), jnp.concatenate(dos[2 * g:2 * g + 2], axis=0))
                    dk_acc[keys, cols[g]] += mm(jnp.concatenate([soft[h - 1][1], soft[h][1]], axis=1), jnp.concatenate(qs[2 * g:2 * g + 2], axis=0))
            for h in range(AHEADB):
                score(h)
            for h in heads:
                score(h + AHEADB)
                soften(h)
                if h >= BEHINDB:
                    mix(h - BEHINDB)
            for h in heads[len(heads) - BEHINDB:] if BEHINDB else ():
                mix(h)
            return tuple(out)
        carry = tuple(jnp.zeros((64, BQ), F32) for _ in range(2 * groups))
        carry = lax.fori_loop(lo_ref[b], b, lambda kb, c: step(kb, c, False), carry)
        carry = step(b, carry, True)
        cos, sin = cos_ref[:, rows], sin_ref[:, rows]
        wide, low, high = rotary_lanes(cos, sin)
        for g in range(groups):
            turned = []
            for w in carry[2 * g:2 * g + 2]:
                turned += [w[:8] * cos + w[8:16] * sin, w[8:16] * cos - w[:8] * sin, w[16:]]
            dq_ref[rows, cols[g]] = (jnp.transpose(jnp.concatenate(turned, axis=0)) * 0.125).astype(BF)
            dk = dk_acc[rows, cols[g]]
            dk = dk * wide - pltpu.roll(dk, PAIR - 8, 1) * low - pltpu.roll(dk, 8, 1) * high
            dk_ref[rows, cols[g]] = dk.astype(BF)
            dv_ref[rows, cols[g]] = dv_acc[rows, cols[g]].astype(BF)
        return 0
    lax.fori_loop(0, nq, q_block, 0)

def attn_bwd(group, index, lo, starts, q, k, v, o, do, lse, cos, sin):
    length = q.shape[0]
    nq = length // BQ
    col = pl.BlockSpec((length, group), lambda p, *_: (0, index))
    own = pl.BlockSpec((length, group), lambda p, *_: (0, 0))
    whole = pl.BlockSpec((ROT // 2, length), lambda p, *_: (0, 0))
    return pl.pallas_call(
        bwd_kernel,
        grid_spec=pltpu.PrefetchScalarGridSpec(
            num_scalar_prefetch=1, grid=(1,),
            in_specs=[pl.BlockSpec((nq, BQ), lambda p, *_: (0, 0)), col, col, col, col, col,
                      pl.BlockSpec((group // 64, nq, BQ), lambda p, *_: (index, 0, 0)), whole, whole],
            out_specs=[own, own, own],
            scratch_shapes=[pltpu.VMEM((length // BK, group, BK), BF), pltpu.VMEM((length, group), F32), pltpu.VMEM((length, group), F32)],
        ),
        out_shape=[jax.ShapeDtypeStruct((length, group), BF)] * 3,
        compiler_params=pltpu.CompilerParams(vmem_limit_bytes=VMEM),
        cost_estimate=COST,
        name="attention_backward",
    )(lo, starts, q, k, v, o, do, lse, cos, sin)

T = 512
TT = 512


def norm_rows(x, eps=NORM_EPS):
    centred = x - jnp.mean(x, axis=-1, keepdims=True)
    root_inv = lax.rsqrt(jnp.mean(centred * centred, axis=-1, keepdims=True) + eps)
    return centred * root_inv, root_inv


def fold_rows(v):
    return jnp.sum(v.reshape(v.shape[0] // 8, 8, v.shape[1]), axis=0)


def project_kernel(x_ref, gain_ref, shift_ref, gain2_ref, shift2_ref, w_ref, b_ref, cos_ref, sin_ref, q_ref, k_ref, v_ref, n1t_ref, n2_ref, n2t_ref):
    local = q_ref.shape[1]
    xhat, _ = norm_rows(x_ref[...].astype(F32))
    normed = (xhat * gain_ref[...] + shift_ref[...]).astype(BF)
    n1t_ref[...] = jnp.transpose(normed)
    normed2 = (xhat * gain2_ref[...] + shift2_ref[...]).astype(BF)
    n2_ref[...] = normed2
    n2t_ref[...] = jnp.transpose(normed2)
    wide, low, high = rotary_lanes(cos_ref[...], sin_ref[...])
    for which, out in enumerate((q_ref, k_ref, v_ref)):
        span = slice(which * local, which * local + local)
        y = mm(normed, w_ref[:, span]) + b_ref[:, span]
        if which == 2:
            out[...] = y.astype(BF)
            continue
        for c in range(local // PAIR):
            cols = slice(c * PAIR, c * PAIR + PAIR)
            u = y[:, cols]
            u = u * wide + pltpu.roll(u, PAIR - 8, 1) * low + pltpu.roll(u, 8, 1) * high
            out[:, cols] = (u * 0.125 if which == 0 else u).astype(BF)


def fixed(shape):
    return pl.BlockSpec(shape, lambda i, *_: (0,) * len(shape), pipeline_mode=pl.Buffered(1))


def tokens(rows, cols):
    return pl.BlockSpec((rows, cols), lambda i, *_: (i, 0))


def across(rows, cols):
    return pl.BlockSpec((rows, cols), lambda i, *_: (0, i))


def project(x, gain, shift, gain2, shift2, w, b, cos, sin):
    length, width = x.shape
    local = w.shape[1] // 3
    return pl.pallas_call(
        project_kernel,
        grid=(length // T,),
        in_specs=[tokens(T, width)] + [fixed((1, width))] * 4 + [fixed(w.shape), fixed(b.shape)] + [across(ROT // 2, T)] * 2,
        out_specs=[tokens(T, local)] * 3 + [across(width, T), tokens(T, width), across(width, T)],
        out_shape=[jax.ShapeDtypeStruct(s, BF) for s in ((length, local),) * 3 + ((width, length), (length, width), (width, length))],
        compiler_params=pltpu.CompilerParams(vmem_limit_bytes=VMEM),
        cost_estimate=COST,
        name="project_qkv",
    )(x, gain, shift, gain2, shift2, w, b, cos, sin)


def scatter_pieces(total, me, outs):
    ranks, local = len(outs), outs[0].shape[1]
    for d in range(ranks):
        target = lax.rem(me + d, ranks)
        cols = pl.ds(pl.multiple_of(target * local, 128), local)
        outs[d][...] = total[:, cols].astype(outs[d].dtype)


def feedforward_kernel(ranks, part, parts, me_ref, n2_ref, n2t_ref, w1_ref, b1_ref, w2_ref, *refs):
    first, last = part == 0, part == parts - 1
    pieces, refs = refs[:ranks], refs[ranks:]
    if first:
        (wd_ref, mixed_ref), refs = refs[:2], refs[2:]
    else:
        (total_in, back_in), refs = refs[:2], refs[2:]
    if last:
        (x_ref,), refs = refs[:1], refs[1:]
        outs, refs = refs[:ranks], refs[ranks:]
        (n2g_ref, lng_ref, lnb_ref), refs = refs[:3], refs[3:]
        sums = [lng_ref, lnb_ref]
    else:
        (total_out, back_out), refs = refs[:2], refs[2:]
        sums = []
    if first:
        (w1_out, w2_out), refs = refs[:2], refs[2:]
    else:
        w1_out, w2_out, refs = refs[0].at[0], refs[0].at[1], refs[1:]
    (b1g_ref,), refs = refs[:1], refs[1:]
    if first:
        (mixed_grad_ref, wd_out), refs = refs[:2], refs[2:]
        (wdg_ref,), refs = refs[:1], refs[1:]
        sums.append(wdg_ref)
    w1g_ref, w2g_ref, g_ref, total_ref, back_ref = refs
    step = pl.program_id(0)
    me = me_ref[0]
    local = pieces[0].shape[1]
    hidden_units = w1_ref.shape[1]
    chunk = min(512, hidden_units)
    chunks = hidden_units // chunk

    @pl.when(step == 0)
    def _():
        for ref in [w1g_ref, w2g_ref, b1g_ref] + sums:
            ref[...] = jnp.zeros_like(ref)

    for d in range(ranks):
        source = lax.rem(me + d, ranks)
        g_ref[:, pl.ds(pl.multiple_of(source * local, 128), local)] = pieces[d][...]
    normed = n2_ref[...]
    g = g_ref[...]
    raw, soft = {}, {}

    def expand(c):
        if c < chunks:
            cols = slice(c * chunk, c * chunk + chunk)
            raw[c] = (mm(normed, w1_ref[:, cols]) + b1_ref[:, cols], mm(g, w2_ref[cols, :], NT))

    def bend(c):
        cols = slice(c * chunk, c * chunk + chunk)
        hidden, active_grad = raw[c]
        cumulative = 0.5 * (1.0 + lax.erf(hidden * 0.7071067811865476))
        density = jnp.exp(-0.5 * hidden * hidden) * 0.3989422804014327
        active = (hidden * cumulative).astype(BF)
        hidden_grad = (active_grad * (cumulative + hidden * density)).astype(BF)
        b1g_ref[:, cols] += fold_rows(hidden_grad.astype(F32))
        soft[c] = (active, hidden_grad)

    def contract(c):
        cols = slice(c * chunk, c * chunk + chunk)
        active, hidden_grad = soft[c]
        feed = mm(active, w2_ref[cols, :])
        back = mm(hidden_grad, w1_ref[:, cols], NT)
        if c == 0 and first:
            total_ref[...] = feed
            back_ref[...] = back
        elif c == 0:
            total_ref[...] = total_in[...] + feed
            back_ref[...] = back_in[...] + back
        else:
            total_ref[...] += feed
            back_ref[...] += back
        w2g_ref[cols, :] += mm(active, g, TN)
        w1g_ref[:, cols] += mm(n2t_ref[...], hidden_grad)

    expand(0)
    for c in range(chunks):
        expand(c + 1)
        bend(c)
        if c >= 1:
            contract(c - 1)
    if first:
        mixed = mixed_ref[...]
        mixed_grad_ref[...] = mm(g, wd_ref[...], NT).astype(BF)
        wdg_ref[...] += mm(mixed, g, TN)
    contract(chunks - 1)
    if first:
        total_ref[...] += mm(mixed, wd_ref[...])
    if last:
        xhat, _ = norm_rows(x_ref[...].astype(F32))
        back = back_ref[...]
        n2g_ref[...] = back.astype(BF)
        lnb_ref[...] += fold_rows(back)
        lng_ref[...] += fold_rows(back * xhat)
        scatter_pieces(total_ref, me, outs)
    else:
        total_out[...] = total_ref[...]
        back_out[...] = back_ref[...]

    @pl.when(step == pl.num_programs(0) - 1)
    def _():
        w1_out[...] = w1g_ref[...].astype(BF)
        w2_out[...] = w2g_ref[...].astype(BF)
        if first:
            wd_out[...] = wdg_ref[...].astype(BF)


def feedforward(part, parts, me, x, n2, n2t, w1, b1, w2, wd, mixed, pieces, carried):
    length, width = x.shape
    local, ranks = pieces[0].shape[1], len(pieces)
    units = w1.shape[1] // parts
    first, last = part == 0, part == parts - 1
    lone = dict(pipeline_mode=pl.Buffered(1))
    ins = [n2, n2t, w1, b1, w2, *pieces]
    specs = [
        tokens(TT, width),
        across(width, TT),
        pl.BlockSpec((width, units), lambda i, *_: (0, part), **lone),
        pl.BlockSpec((1, units), lambda i, *_: (0, part), **lone),
        pl.BlockSpec((units, width), lambda i, *_: (part, 0), **lone),
    ] + [tokens(TT, local)] * ranks
    if first:
        ins += [wd, mixed]
        specs += [fixed(wd.shape), tokens(TT, local)]
    else:
        ins += list(carried)
        specs += [tokens(TT, width)] * 2
    outs = []
    if last:
        ins.append(x)
        specs.append(tokens(TT, width))
        outs += [(tokens(TT, local), (length, local), F32)] + [(tokens(TT, local), (length, local), BF)] * (ranks - 1)
        outs += [(tokens(TT, width), (length, width), BF)] + [(fixed((8, width)), (8, width), F32)] * 2
    else:
        outs += [(tokens(TT, width), (length, width), F32)] * 2
    if first:
        outs += [(fixed((width, units)), (width, units), BF), (fixed((units, width)), (units, width), BF)]
    else:
        outs.append((fixed((2, width, units)), (2, width, units), BF))
    outs.append((fixed((8, units)), (8, units), F32))
    scratch = []
    if first:
        outs += [(tokens(TT, local), (length, local), BF), (fixed((local, width)), (local, width), BF)]
        scratch.append(pltpu.VMEM((local, width), F32))
    scratch += [pltpu.VMEM((width, units), F32), pltpu.VMEM((units, width), F32), pltpu.VMEM((TT, width), BF), pltpu.VMEM((TT, width), F32), pltpu.VMEM((TT, width), F32)]
    made = pl.pallas_call(
        functools.partial(feedforward_kernel, ranks, part, parts),
        grid_spec=pltpu.PrefetchScalarGridSpec(
            num_scalar_prefetch=1,
            grid=(length // TT,),
            in_specs=specs,
            out_specs=[o[0] for o in outs],
            scratch_shapes=scratch,
        ),
        out_shape=[jax.ShapeDtypeStruct(o[1], o[2]) for o in outs],
        compiler_params=pltpu.CompilerParams(vmem_limit_bytes=VMEM),
        cost_estimate=COST,
        name="feedforward_both_ways",
    )(me, *ins)
    made = list(made)
    result = {}
    if last:
        result["outs"], made = made[:ranks], made[ranks:]
        result["n2g"], result["ln2g"], result["ln2b"] = made[:3]
        made = made[3:]
    else:
        result["carried"], made = made[:2], made[2:]
    if first:
        result["w1g"], result["w2g"], result["b1g"], result["mixed_grad"], result["wdg"] = made
    else:
        result["both"], result["b1g"] = made
    return result


def weights_kernel(n1t_ref, dq_ref, dk_ref, dv_ref, out_ref, bg_ref, acc_ref):
    step = pl.program_id(0)

    @pl.when(step == 0)
    def _():
        acc_ref[...] = jnp.zeros_like(acc_ref)
        bg_ref[...] = jnp.zeros_like(bg_ref)

    n1t = n1t_ref[...]
    for which, ref in enumerate((dq_ref, dk_ref, dv_ref)):
        acc_ref[which] += mm(n1t, ref[...])
        bg_ref[which] += fold_rows(ref[...].astype(F32))

    @pl.when(step == pl.num_programs(0) - 1)
    def _():
        out_ref[...] = acc_ref[...].astype(BF)


def weights_backward(index, group, n1t, dq, dk, dv):
    width, length = n1t.shape
    rows = 1024
    return pl.pallas_call(
        weights_kernel,
        grid=(length // rows,),
        in_specs=[across(width, rows)] + [pl.BlockSpec((rows, group), lambda i: (i, index))] * 3,
        out_specs=[fixed((3, width, group)), fixed((3, 8, group))],
        out_shape=[jax.ShapeDtypeStruct((3, width, group), BF), jax.ShapeDtypeStruct((3, 8, group), F32)],
        scratch_shapes=[pltpu.VMEM((3, width, group), F32)],
        compiler_params=pltpu.CompilerParams(vmem_limit_bytes=VMEM),
        cost_estimate=COST,
        name="qkv_weights_backward",
    )(n1t, dq, dk, dv)


def input_kernel(ranks, groups, me_ref, x_ref, gain1_ref, gain2_ref, w_ref, n2g_ref, *refs):
    grads, refs = refs[:3 * groups], refs[3 * groups:]
    outs, refs = refs[:ranks], refs[ranks:]
    lng_ref, lnb_ref, total_ref = refs
    group = grads[0].shape[1]

    @pl.when(pl.program_id(0) == 0)
    def _():
        lng_ref[...] = jnp.zeros_like(lng_ref)
        lnb_ref[...] = jnp.zeros_like(lnb_ref)

    back = None
    for which in range(3):
        for c in range(groups):
            first = (which * groups + c) * group
            term = mm(grads[3 * c + which][...], w_ref[:, first:first + group], NT)
            back = term if back is None else back + term
    xhat, root_inv = norm_rows(x_ref[...].astype(F32))
    lnb_ref[...] += fold_rows(back)
    lng_ref[...] += fold_rows(back * xhat)
    e = back * gain1_ref[...] + n2g_ref[...].astype(F32) * gain2_ref[...]
    total_ref[...] = root_inv * (e - jnp.mean(e, axis=-1, keepdims=True) - xhat * jnp.mean(e * xhat, axis=-1, keepdims=True))
    scatter_pieces(total_ref, me_ref[0], outs)


def input_backward(start, rows, me, ranks, x, gain1, gain2, w, n2g, grads):
    width = x.shape[1]
    group = grads[0].shape[1]
    local = w.shape[1] // 3
    shift = start // T
    piece = lambda cols: pl.BlockSpec((T, cols), lambda i, *_: (i + shift, 0))
    shapes = [((rows, local), F32)] + [((rows, local), BF)] * (ranks - 1)
    return pl.pallas_call(
        functools.partial(input_kernel, ranks, len(grads) // 3),
        grid_spec=pltpu.PrefetchScalarGridSpec(
            num_scalar_prefetch=1,
            grid=(rows // T,),
            in_specs=[piece(width), fixed((1, width)), fixed((1, width)), fixed(w.shape), piece(width)] + [piece(group)] * len(grads),
            out_specs=[tokens(T, s[1]) for s, _ in shapes] + [fixed((8, width))] * 2,
            scratch_shapes=[pltpu.VMEM((T, width), F32)],
        ),
        out_shape=[jax.ShapeDtypeStruct(s, d) for s, d in shapes] + [jax.ShapeDtypeStruct((8, width), F32)] * 2,
        compiler_params=pltpu.CompilerParams(vmem_limit_bytes=VMEM),
        cost_estimate=COST,
        name="input_backward",
    )(me, x, gain1, gain2, w, n2g, *grads)


def rotary_tables(segments):
    length = segments.shape[0]
    places = jnp.arange(length, dtype=jnp.int32)
    first = jnp.concatenate([jnp.ones((1,), dtype=bool), segments[1:] != segments[:-1]])
    starts = lax.cummax(jnp.where(first, places, jnp.zeros_like(places)), axis=0)
    offsets = (places - starts).astype(F32)
    inverse = 10000.0 ** (-jnp.arange(0, ROT, 2).astype(F32) / ROT)
    angles = inverse[:, None] * offsets[None, :]
    return starts, jnp.cos(angles), jnp.sin(angles)


def tie(value, *others):
    return lax.optimization_barrier((value, *others))[0]


def shifted(ranks, distance):
    return [(i, (i + distance) % ranks) for i in range(ranks)]


def send_pieces(pieces):
    ranks = len(pieces)
    came = [lax.ppermute(pieces[d], "tensor", shifted(ranks, d)) for d in range(1, ranks)]
    return sum([c.astype(F32) for c in came], pieces[0]), came


def swap_sum(value, axis, ranks):
    step = 1
    while step < ranks:
        value = value + lax.ppermute(value, axis, [(i, i ^ step) for i in range(ranks)])
        step *= 2
    return value


def halve_sum(value, packs, step):
    bit = (lax.axis_index("dp") // step) % 2
    half = value.shape[0] // 2
    sent = lax.dynamic_slice_in_dim(value, (1 - bit) * half, half, 0).astype(BF)
    kept = lax.dynamic_slice_in_dim(value, bit * half, half, 0).astype(F32)
    return kept + lax.ppermute(sent, "dp", [(i, i ^ step) for i in range(packs)]).astype(F32)


def double(value, packs, step):
    bit = (lax.axis_index("dp") // step) % 2
    other = lax.ppermute(value, "dp", [(i, i ^ step) for i in range(packs)])
    return jnp.where(bit == 0, jnp.concatenate([value, other], axis=0), jnp.concatenate([other, value], axis=0))


def far_shift(packs, far, distance):
    return [(i, ((i // far + distance) * far) % packs + i % far) for i in range(packs)]


def far_sum(value, packs, far):
    count = packs // far
    place = lax.axis_index("dp") // far
    part = value.shape[0] // count
    total = lax.dynamic_slice_in_dim(value, place * part, part, 0)
    for d in range(1, count):
        sent = lax.dynamic_slice_in_dim(value, ((place + d) % count) * part, part, 0).astype(BF)
        total = total + lax.ppermute(sent, "dp", far_shift(packs, far, d)).astype(F32)
    return total


def far_gather(value, packs, far):
    count = packs // far
    place = lax.axis_index("dp") // far
    part = value.shape[0]
    whole = jnp.zeros((count * part,) + value.shape[1:], value.dtype)
    whole = lax.dynamic_update_slice_in_dim(whole, value, place * part, 0)
    for d in range(1, count):
        came = lax.ppermute(value, "dp", far_shift(packs, far, d))
        whole = lax.dynamic_update_slice_in_dim(whole, came, ((place + count - d) % count) * part, 0)
    return whole


def on_device(sizes, inputs, segment_ids, cotangent, ln1_gain, attention_norm_bias, ln2_gain, feedforward_norm_bias, w_qkv, b_qkv, w_dense, b_dense, w_fc1, b_fc1, w_fc2, b_fc2):
    packs, ranks = sizes
    segments = segment_ids[0]
    length, width = inputs.shape
    local = w_qkv.shape[2]
    me = lax.axis_index("tensor").astype(jnp.int32).reshape(1)
    pieces = [cotangent] + [lax.ppermute(cotangent, "tensor", shifted(ranks, ranks - d)) for d in range(1, ranks)]
    starts, cosine, sine = rotary_tables(segments)
    starts = starts.reshape(-1, BQ)
    lowest = starts[:, 0] // BK
    row = lambda v: v.astype(F32).reshape(1, -1)
    qkv_matrix = w_qkv.reshape(width, 3 * local)
    gain1, gain2 = row(ln1_gain), row(ln2_gain)
    shift1, shift2 = row(attention_norm_bias), row(feedforward_norm_bias)
    query, key, value, n1t, n2, n2t = project(inputs, gain1, shift1, gain2, shift2, qkv_matrix, row(b_qkv), cosine, sine)
    mixed, totals = attn_fwd(lowest, starts, query, key, value)
    parts = 2 if w_fc1.shape[1] == 2 * width else 1
    made, carried = [], None
    for part in range(parts):
        made.append(feedforward(part, parts, me, inputs, n2, n2t, w_fc1, row(b_fc1), w_fc2, w_dense, mixed, pieces, carried))
        carried = made[-1].get("carried")
    early = lax.psum((made[0]["w1g"], made[0]["w2g"], made[0]["wdg"]), "dp")
    late = [lax.psum_scatter(m["both"].reshape(2 * width, width), "dp", scatter_dimension=0, tiled=True) for m in made[1:]]
    own = lax.dynamic_slice_in_dim(inputs, me[0] * local, local, 1).astype(F32)
    outputs = (send_pieces(made[-1]["outs"])[0] + own + b_dense.astype(F32) + b_fc2.astype(F32)).astype(BF)
    grads = attn_bwd(min(GB * PAIR, local), 0, lowest, starts, query, key, value, mixed, made[0]["mixed_grad"], totals, cosine, sine)
    group = min(2 * PAIR, local)
    groups = local // group
    count = 3 if length % (3 * T) == 0 else 1
    rows = length // count
    weights, biases, input_grad, norms, arrived = [], [], [], [], []
    n1t = tie(n1t, grads[0], *early)
    for c in range(groups):
        wg, bg = weights_backward(c, group, n1t, *grads)
        wg = halve_sum(wg.reshape(3 * width, group), packs, 1)
        n1t = tie(n1t, wg)
        biases.append(jnp.sum(bg, axis=1))
        weights.append(halve_sum(wg, packs, 2))
    normed2_grad = tie(made[-1]["n2g"], n1t, outputs, *weights[:-1])
    for c in range(count):
        got = input_backward(c * rows, rows, me, ranks, inputs, gain1, gain2, qkv_matrix, normed2_grad, grads)
        total, came = send_pieces(got[:ranks])
        arrived += came[:1]
        input_grad.append(total + cotangent[c * rows : c * rows + rows].astype(F32))
        norms.append(jnp.stack([jnp.sum(v, axis=0) for v in got[ranks:]]))
        if c == 0:
            normed2_grad = tie(normed2_grad, got[0], *weights)
            wg = far_sum(jnp.concatenate(weights, axis=1), packs, 4).astype(BF)
        if c == 1:
            normed2_grad = tie(normed2_grad, got[0], wg)
            wg = far_gather(wg, packs, 4)
    if count == 1:
        wg = far_gather(wg, packs, 4)
    norms[-1] = tie(norms[-1], *arrived[:2], *late)
    late = lax.optimization_barrier((*late, got[0]))[:-1]
    late = [lax.all_gather(v, "dp", axis=0, tiled=True) for v in late]
    input_grad = jnp.concatenate(input_grad, axis=0)
    wg = double(double(wg, packs, 2), packs, 1).astype(F32)
    qkv_weight_grad = wg.reshape(3, width, local).transpose(1, 0, 2)
    norms = jnp.concatenate([sum(norms)] + [jnp.sum(made[-1][n], axis=0, keepdims=True) for n in ("ln2g", "ln2b")], axis=0)
    out_bias = jnp.sum(cotangent.astype(F32), axis=0)
    b1g = [jnp.sum(m["b1g"], axis=0) for m in made]
    bias = jnp.concatenate(biases, axis=1).reshape(-1)
    small = jnp.concatenate([norms.reshape(-1), out_bias, bias] + b1g).reshape(-1, 128)
    small = swap_sum(small, "dp", packs).reshape(-1)
    norms, small = small[: 4 * width].reshape(4, width), small[4 * width :]
    norms = swap_sum(norms, "tensor", ranks)
    dense_bias_grad, small = small[:local], small[local:]
    qkv_bias_grad, fc1_bias_grad = small[: 3 * local].reshape(3, local), small[3 * local :]
    w1g = [v.astype(F32) for v in [early[0]] + [v[:width] for v in late]]
    w2g = [v.astype(F32) for v in [early[1]] + [v[width:] for v in late]]
    return (
        outputs,
        input_grad,
        norms[0],
        norms[1],
        norms[2],
        norms[3],
        qkv_weight_grad,
        qkv_bias_grad,
        early[2].astype(F32),
        dense_bias_grad,
        jnp.concatenate(w1g, axis=1),
        fc1_bias_grad,
        jnp.concatenate(w2g, axis=0),
        dense_bias_grad,
    )


def solution(mesh):
    placed = (
        P("dp", None),
        P("dp", None),
        P("dp", "tensor"),
        P(),
        P(),
        P(),
        P(),
        P(None, None, "tensor"),
        P(None, "tensor"),
        P("tensor", None),
        P("tensor"),
        P(None, "tensor"),
        P("tensor"),
        P("tensor", None),
        P("tensor"),
    )
    sizes = (mesh.shape["dp"], mesh.shape["tensor"])
    return jax.shard_map(
        functools.partial(on_device, sizes),
        mesh=mesh,
        in_specs=placed,
        out_specs=(
            P("dp", "tensor"),
            P("dp", "tensor"),
            P(),
            P(),
            P(),
            P(),
            P(None, None, "tensor"),
            P(None, "tensor"),
            P("tensor", None),
            P("tensor"),
            P(None, "tensor"),
            P("tensor"),
            P("tensor", None),
            P("tensor"),
        ),
        check_vma=False,
    )
```

```python
import functools

import jax
import jax.numpy as jnp
from jax import lax
from jax.experimental import pallas as pl
from jax.experimental.pallas import tpu as pltpu
from jax.sharding import PartitionSpec as P

BQ = 256
BK = 256
PAIR = 128
NEG = -1e30
ROT = 16
NORM_EPS = 1e-05
VMEM = 60 * 1024 * 1024
COST = pl.CostEstimate(flops=1, bytes_accessed=1, transcendentals=0)
GF = 4
GB = 4
AHEAD = 2
BEHIND = 2
AHEADB = 2
BEHINDB = 1
F32 = jnp.float32
BF = jnp.bfloat16
NT = (((1,), (1,)), ((), ()))
NN = (((1,), (0,)), ((), ()))
TN = (((0,), (0,)), ((), ()))

def mm(a, b, dims=NN):
    return lax.dot_general(a, b, dims, preferred_element_type=F32)

def rotary_lanes(cos, sin):
    rest = jnp.ones((64 - ROT, cos.shape[1]), F32)
    none = jnp.zeros((64 - ROT, cos.shape[1]), F32)
    blank = jnp.zeros_like(cos)
    wide = jnp.concatenate([cos, cos, rest] * 2, axis=0)
    low = jnp.concatenate([-sin, blank, none] * 2, axis=0)
    high = jnp.concatenate([blank, sin, none] * 2, axis=0)
    return jnp.transpose(wide), jnp.transpose(low), jnp.transpose(high)


def lane_half(shape):
    return lax.broadcasted_iota(jnp.int32, shape, 1) < 64

def fwd_kernel(lo_ref, start_ref, q_ref, k_ref, v_ref, o_ref, lse_ref, vt_ref):
    length = q_ref.shape[0]
    nq = length // BQ
    nk = length // BK
    groups = q_ref.shape[1] // PAIR
    for i in range(nk):
        vt_ref[i] = jnp.transpose(v_ref[i * BK:(i + 1) * BK, :])
    first = lane_half((BQ, PAIR))

    def q_block(b, _):
        rows = pl.ds(pl.multiple_of(b * BQ, BQ), BQ)
        qs = []
        for g in range(groups):
            q = q_ref[rows, PAIR * g:PAIR * g + PAIR]
            zero = jnp.zeros_like(q)
            qs += [jnp.where(first, q, zero), jnp.where(first, zero, q)]
        starts = start_ref[pl.ds(b, 1), :]
        def step(kb, carry, diagonal):
            keys = pl.ds(pl.multiple_of(kb * BK, BK), BK)
            place = lax.broadcasted_iota(jnp.int32, (BK, BQ), 0)
            allowed = place >= starts - kb * BK
            if diagonal:
                allowed = allowed & (place <= lax.broadcasted_iota(jnp.int32, (BK, BQ), 1))
            heads = range(2 * groups)
            scores, weights, out = {}, {}, []
            def score(h):
                if h in heads:
                    k = k_ref[keys, PAIR * (h // 2):PAIR * (h // 2) + PAIR]
                    scores[h] = mm(k, qs[h], NT)
            def soften(h):
                m, l, acc = carry[h]
                s = jnp.where(allowed, scores[h], NEG)
                m_new = jnp.maximum(m, jnp.max(s, axis=0, keepdims=True))
                p = jnp.exp(s - m_new)
                alpha = jnp.exp(m - m_new)
                weights[h] = (m_new, l * alpha + jnp.sum(p, axis=0, keepdims=True), alpha, p.astype(BF))
            def mix(h):
                m_new, l, alpha, p = weights[h]
                out.append((m_new, l, carry[h][2] * alpha + mm(vt_ref[kb, 64 * h:64 * h + 64, :], p)))
            for h in range(AHEAD):
                score(h)
            for h in heads:
                score(h + AHEAD)
                soften(h)
                if h >= BEHIND:
                    mix(h - BEHIND)
            for h in heads[len(heads) - BEHIND:] if BEHIND else ():
                mix(h)
            return tuple(out)
        init = tuple((jnp.full((1, BQ), NEG, F32), jnp.zeros((1, BQ), F32), jnp.zeros((64, BQ), F32)) for _ in range(2 * groups))
        carry = step(b, init, True)
        carry = lax.fori_loop(lo_ref[b], b, lambda kb, c: step(kb, c, False), carry)
        for h in range(2 * groups):
            lse_ref[h, pl.ds(b, 1), :] = carry[h][0] + jnp.log(carry[h][1])
        ot = jnp.concatenate([c[2] / c[1] for c in carry], axis=0)
        o_ref[rows, :] = jnp.transpose(ot).astype(BF)
        return 0
    lax.fori_loop(0, nq, q_block, 0)

def attn_fwd(lo, starts, q, k, v):
    length, width = q.shape
    nq = length // BQ
    group = min(GF * PAIR, width)
    pairs = width // group
    col = pl.BlockSpec((length, group), lambda p, *_: (0, p))
    return pl.pallas_call(
        fwd_kernel,
        grid_spec=pltpu.PrefetchScalarGridSpec(
            num_scalar_prefetch=1, grid=(pairs,),
            in_specs=[pl.BlockSpec((nq, BQ), lambda p, *_: (0, 0)), col, col, col],
            out_specs=[col, pl.BlockSpec((group // 64, nq, BQ), lambda p, *_: (p, 0, 0))],
            scratch_shapes=[pltpu.VMEM((length // BK, group, BK), BF)],
        ),
        out_shape=[jax.ShapeDtypeStruct((length, width), BF), jax.ShapeDtypeStruct((width // 64, nq, BQ), F32)],
        compiler_params=pltpu.CompilerParams(vmem_limit_bytes=VMEM),
        cost_estimate=COST,
        name="attention_forward",
    )(lo, starts, q, k, v)

def bwd_kernel(lo_ref, start_ref, q_ref, k_ref, v_ref, o_ref, do_ref, lse_ref, cos_ref, sin_ref, dq_ref, dk_ref, dv_ref, kt_ref, dk_acc, dv_acc):
    length = q_ref.shape[0]
    nq = length // BQ
    nk = length // BK
    groups = q_ref.shape[1] // PAIR
    for i in range(nk):
        kt_ref[i] = jnp.transpose(k_ref[i * BK:(i + 1) * BK, :])
    first = lane_half((BQ, PAIR))
    dk_acc[...] = jnp.zeros_like(dk_acc)
    dv_acc[...] = jnp.zeros_like(dv_acc)

    cols = [slice(PAIR * g, PAIR * g + PAIR) for g in range(groups)]

    def q_block(step_index, _):
        b = nq - 1 - step_index
        rows = pl.ds(pl.multiple_of(b * BQ, BQ), BQ)
        starts = start_ref[pl.ds(b, 1), :]
        qs, dos, deltas, lses = [], [], [], []
        for g in range(groups):
            q = q_ref[rows, cols[g]]
            do = do_ref[rows, cols[g]]
            zero = jnp.zeros_like(q)
            qs += [jnp.where(first, q, zero), jnp.where(first, zero, q)]
            dos += [jnp.where(first, do, zero), jnp.where(first, zero, do)]
            prod = jnp.transpose(do.astype(F32) * o_ref[rows, cols[g]].astype(F32))
            deltas += [jnp.sum(prod[:64], axis=0, keepdims=True), jnp.sum(prod[64:], axis=0, keepdims=True)]
            lses += [lse_ref[2 * g, pl.ds(b, 1), :], lse_ref[2 * g + 1, pl.ds(b, 1), :]]
        def step(kb, carry, diagonal):
            keys = pl.ds(pl.multiple_of(kb * BK, BK), BK)
            place = lax.broadcasted_iota(jnp.int32, (BK, BQ), 0)
            allowed = place >= starts - kb * BK
            if diagonal:
                allowed = allowed & (place <= lax.broadcasted_iota(jnp.int32, (BK, BQ), 1))
            out = []
            heads = range(2 * groups)
            raw, soft = {}, {}
            def score(h):
                if h in heads:
                    raw[h] = (mm(k_ref[keys, cols[h // 2]], qs[h], NT), mm(v_ref[keys, cols[h // 2]], dos[h], NT))
            def soften(h):
                s, dp = raw[h]
                p = jnp.exp(jnp.where(allowed, s - lses[h], NEG))
                soft[h] = (p.astype(BF), (p * (dp - deltas[h])).astype(BF))
            def mix(h):
                out.append(carry[h] + mm(kt_ref[kb, 64 * h:64 * h + 64, :], soft[h][1]))
                if h % 2 == 1:
                    g = h // 2
                    dv_acc[keys, cols[g]] += mm(jnp.concatenate([soft[h - 1][0], soft[h][0]], axis=1), jnp.concatenate(dos[2 * g:2 * g + 2], axis=0))
                    dk_acc[keys, cols[g]] += mm(jnp.concatenate([soft[h - 1][1], soft[h][1]], axis=1), jnp.concatenate(qs[2 * g:2 * g + 2], axis=0))
            for h in range(AHEADB):
                score(h)
            for h in heads:
                score(h + AHEADB)
                soften(h)
                if h >= BEHINDB:
                    mix(h - BEHINDB)
            for h in heads[len(heads) - BEHINDB:] if BEHINDB else ():
                mix(h)
            return tuple(out)
        carry = tuple(jnp.zeros((64, BQ), F32) for _ in range(2 * groups))
        carry = lax.fori_loop(lo_ref[b], b, lambda kb, c: step(kb, c, False), carry)
        carry = step(b, carry, True)
        cos, sin = cos_ref[:, rows], sin_ref[:, rows]
        wide, low, high = rotary_lanes(cos, sin)
        for g in range(groups):
            turned = []
            for w in carry[2 * g:2 * g + 2]:
                turned += [w[:8] * cos + w[8:16] * sin, w[8:16] * cos - w[:8] * sin, w[16:]]
            dq_ref[rows, cols[g]] = (jnp.transpose(jnp.concatenate(turned, axis=0)) * 0.125).astype(BF)
            dk = dk_acc[rows, cols[g]]
            dk = dk * wide - pltpu.roll(dk, PAIR - 8, 1) * low - pltpu.roll(dk, 8, 1) * high
            dk_ref[rows, cols[g]] = dk.astype(BF)
            dv_ref[rows, cols[g]] = dv_acc[rows, cols[g]].astype(BF)
        return 0
    lax.fori_loop(0, nq, q_block, 0)

def attn_bwd(group, index, lo, starts, q, k, v, o, do, lse, cos, sin):
    length = q.shape[0]
    nq = length // BQ
    col = pl.BlockSpec((length, group), lambda p, *_: (0, index))
    own = pl.BlockSpec((length, group), lambda p, *_: (0, 0))
    whole = pl.BlockSpec((ROT // 2, length), lambda p, *_: (0, 0))
    return pl.pallas_call(
        bwd_kernel,
        grid_spec=pltpu.PrefetchScalarGridSpec(
            num_scalar_prefetch=1, grid=(1,),
            in_specs=[pl.BlockSpec((nq, BQ), lambda p, *_: (0, 0)), col, col, col, col, col,
                      pl.BlockSpec((group // 64, nq, BQ), lambda p, *_: (index, 0, 0)), whole, whole],
            out_specs=[own, own, own],
            scratch_shapes=[pltpu.VMEM((length // BK, group, BK), BF), pltpu.VMEM((length, group), F32), pltpu.VMEM((length, group), F32)],
        ),
        out_shape=[jax.ShapeDtypeStruct((length, group), BF)] * 3,
        compiler_params=pltpu.CompilerParams(vmem_limit_bytes=VMEM),
        cost_estimate=COST,
        name="attention_backward",
    )(lo, starts, q, k, v, o, do, lse, cos, sin)

T = 512
TT = 512


def norm_rows(x, eps=NORM_EPS):
    centred = x - jnp.mean(x, axis=-1, keepdims=True)
    root_inv = lax.rsqrt(jnp.mean(centred * centred, axis=-1, keepdims=True) + eps)
    return centred * root_inv, root_inv


def fold_rows(v):
    return jnp.sum(v.reshape(v.shape[0] // 8, 8, v.shape[1]), axis=0)


def project_kernel(x_ref, gain_ref, shift_ref, gain2_ref, shift2_ref, w_ref, b_ref, cos_ref, sin_ref, q_ref, k_ref, v_ref, n1t_ref, n2_ref, n2t_ref):
    local = q_ref.shape[1]
    xhat, _ = norm_rows(x_ref[...].astype(F32))
    normed = (xhat * gain_ref[...] + shift_ref[...]).astype(BF)
    n1t_ref[...] = jnp.transpose(normed)
    normed2 = (xhat * gain2_ref[...] + shift2_ref[...]).astype(BF)
    n2_ref[...] = normed2
    n2t_ref[...] = jnp.transpose(normed2)
    wide, low, high = rotary_lanes(cos_ref[...], sin_ref[...])
    for which, out in enumerate((q_ref, k_ref, v_ref)):
        span = slice(which * local, which * local + local)
        y = mm(normed, w_ref[:, span]) + b_ref[:, span]
        if which == 2:
            out[...] = y.astype(BF)
            continue
        for c in range(local // PAIR):
            cols = slice(c * PAIR, c * PAIR + PAIR)
            u = y[:, cols]
            u = u * wide + pltpu.roll(u, PAIR - 8, 1) * low + pltpu.roll(u, 8, 1) * high
            out[:, cols] = (u * 0.125 if which == 0 else u).astype(BF)


def fixed(shape):
    return pl.BlockSpec(shape, lambda i, *_: (0,) * len(shape), pipeline_mode=pl.Buffered(1))


def tokens(rows, cols):
    return pl.BlockSpec((rows, cols), lambda i, *_: (i, 0))


def across(rows, cols):
    return pl.BlockSpec((rows, cols), lambda i, *_: (0, i))


def project(x, gain, shift, gain2, shift2, w, b, cos, sin):
    length, width = x.shape
    local = w.shape[1] // 3
    return pl.pallas_call(
        project_kernel,
        grid=(length // T,),
        in_specs=[tokens(T, width)] + [fixed((1, width))] * 4 + [fixed(w.shape), fixed(b.shape)] + [across(ROT // 2, T)] * 2,
        out_specs=[tokens(T, local)] * 3 + [across(width, T), tokens(T, width), across(width, T)],
        out_shape=[jax.ShapeDtypeStruct(s, BF) for s in ((length, local),) * 3 + ((width, length), (length, width), (width, length))],
        compiler_params=pltpu.CompilerParams(vmem_limit_bytes=VMEM),
        cost_estimate=COST,
        name="project_qkv",
    )(x, gain, shift, gain2, shift2, w, b, cos, sin)


def scatter_pieces(total, me, outs):
    ranks, local = len(outs), outs[0].shape[1]
    for d in range(ranks):
        target = lax.rem(me + d, ranks)
        cols = pl.ds(pl.multiple_of(target * local, 128), local)
        outs[d][...] = total[:, cols].astype(outs[d].dtype)


def feedforward_kernel(ranks, part, parts, me_ref, n2_ref, n2t_ref, w1_ref, b1_ref, w2_ref, *refs):
    first, last = part == 0, part == parts - 1
    pieces, refs = refs[:ranks], refs[ranks:]
    if first:
        (wd_ref, mixed_ref), refs = refs[:2], refs[2:]
    else:
        (total_in, back_in), refs = refs[:2], refs[2:]
    if last:
        (x_ref,), refs = refs[:1], refs[1:]
        outs, refs = refs[:ranks], refs[ranks:]
        (n2g_ref, lng_ref, lnb_ref), refs = refs[:3], refs[3:]
        sums = [lng_ref, lnb_ref]
    else:
        (total_out, back_out), refs = refs[:2], refs[2:]
        sums = []
    if first:
        (w1_out, w2_out), refs = refs[:2], refs[2:]
    else:
        w1_out, w2_out, refs = refs[0].at[0], refs[0].at[1], refs[1:]
    (b1g_ref,), refs = refs[:1], refs[1:]
    if first:
        (mixed_grad_ref, wd_out), refs = refs[:2], refs[2:]
        (wdg_ref,), refs = refs[:1], refs[1:]
        sums.append(wdg_ref)
    w1g_ref, w2g_ref, g_ref, total_ref, back_ref = refs
    step = pl.program_id(0)
    me = me_ref[0]
    local = pieces[0].shape[1]
    hidden_units = w1_ref.shape[1]
    chunk = min(512, hidden_units)
    chunks = hidden_units // chunk

    @pl.when(step == 0)
    def _():
        for ref in [w1g_ref, w2g_ref, b1g_ref] + sums:
            ref[...] = jnp.zeros_like(ref)

    for d in range(ranks):
        source = lax.rem(me + d, ranks)
        g_ref[:, pl.ds(pl.multiple_of(source * local, 128), local)] = pieces[d][...]
    normed = n2_ref[...]
    g = g_ref[...]
    raw, soft = {}, {}

    def expand(c):
        if c < chunks:
            cols = slice(c * chunk, c * chunk + chunk)
            raw[c] = (mm(normed, w1_ref[:, cols]) + b1_ref[:, cols], mm(g, w2_ref[cols, :], NT))

    def bend(c):
        cols = slice(c * chunk, c * chunk + chunk)
        hidden, active_grad = raw[c]
        cumulative = 0.5 * (1.0 + lax.erf(hidden * 0.7071067811865476))
        density = jnp.exp(-0.5 * hidden * hidden) * 0.3989422804014327
        active = (hidden * cumulative).astype(BF)
        hidden_grad = (active_grad * (cumulative + hidden * density)).astype(BF)
        b1g_ref[:, cols] += fold_rows(hidden_grad.astype(F32))
        soft[c] = (active, hidden_grad)

    def contract(c):
        cols = slice(c * chunk, c * chunk + chunk)
        active, hidden_grad = soft[c]
        feed = mm(active, w2_ref[cols, :])
        back = mm(hidden_grad, w1_ref[:, cols], NT)
        if c == 0 and first:
            total_ref[...] = feed
            back_ref[...] = back
        elif c == 0:
            total_ref[...] = total_in[...] + feed
            back_ref[...] = back_in[...] + back
        else:
            total_ref[...] += feed
            back_ref[...] += back
        w2g_ref[cols, :] += mm(active, g, TN)
        w1g_ref[:, cols] += mm(n2t_ref[...], hidden_grad)

    expand(0)
    for c in range(chunks):
        expand(c + 1)
        bend(c)
        if c >= 1:
            contract(c - 1)
    if first:
        mixed = mixed_ref[...]
        mixed_grad_ref[...] = mm(g, wd_ref[...], NT).astype(BF)
        wdg_ref[...] += mm(mixed, g, TN)
    contract(chunks - 1)
    if first:
        total_ref[...] += mm(mixed, wd_ref[...])
    if last:
        xhat, _ = norm_rows(x_ref[...].astype(F32))
        back = back_ref[...]
        n2g_ref[...] = back.astype(BF)
        lnb_ref[...] += fold_rows(back)
        lng_ref[...] += fold_rows(back * xhat)
        scatter_pieces(total_ref, me, outs)
    else:
        total_out[...] = total_ref[...]
        back_out[...] = back_ref[...]

    @pl.when(step == pl.num_programs(0) - 1)
    def _():
        w1_out[...] = w1g_ref[...].astype(BF)
        w2_out[...] = w2g_ref[...].astype(BF)
        if first:
            wd_out[...] = wdg_ref[...].astype(BF)


def feedforward(part, parts, me, x, n2, n2t, w1, b1, w2, wd, mixed, pieces, carried):
    length, width = x.shape
    local, ranks = pieces[0].shape[1], len(pieces)
    units = w1.shape[1] // parts
    first, last = part == 0, part == parts - 1
    lone = dict(pipeline_mode=pl.Buffered(1))
    ins = [n2, n2t, w1, b1, w2, *pieces]
    specs = [
        tokens(TT, width),
        across(width, TT),
        pl.BlockSpec((width, units), lambda i, *_: (0, part), **lone),
        pl.BlockSpec((1, units), lambda i, *_: (0, part), **lone),
        pl.BlockSpec((units, width), lambda i, *_: (part, 0), **lone),
    ] + [tokens(TT, local)] * ranks
    if first:
        ins += [wd, mixed]
        specs += [fixed(wd.shape), tokens(TT, local)]
    else:
        ins += list(carried)
        specs += [tokens(TT, width)] * 2
    outs = []
    if last:
        ins.append(x)
        specs.append(tokens(TT, width))
        outs += [(tokens(TT, local), (length, local), F32)] + [(tokens(TT, local), (length, local), BF)] * (ranks - 1)
        outs += [(tokens(TT, width), (length, width), BF)] + [(fixed((8, width)), (8, width), F32)] * 2
    else:
        outs += [(tokens(TT, width), (length, width), F32)] * 2
    if first:
        outs += [(fixed((width, units)), (width, units), BF), (fixed((units, width)), (units, width), BF)]
    else:
        outs.append((fixed((2, width, units)), (2, width, units), BF))
    outs.append((fixed((8, units)), (8, units), F32))
    scratch = []
    if first:
        outs += [(tokens(TT, local), (length, local), BF), (fixed((local, width)), (local, width), BF)]
        scratch.append(pltpu.VMEM((local, width), F32))
    scratch += [pltpu.VMEM((width, units), F32), pltpu.VMEM((units, width), F32), pltpu.VMEM((TT, width), BF), pltpu.VMEM((TT, width), F32), pltpu.VMEM((TT, width), F32)]
    made = pl.pallas_call(
        functools.partial(feedforward_kernel, ranks, part, parts),
        grid_spec=pltpu.PrefetchScalarGridSpec(
            num_scalar_prefetch=1,
            grid=(length // TT,),
            in_specs=specs,
            out_specs=[o[0] for o in outs],
            scratch_shapes=scratch,
        ),
        out_shape=[jax.ShapeDtypeStruct(o[1], o[2]) for o in outs],
        compiler_params=pltpu.CompilerParams(vmem_limit_bytes=VMEM),
        cost_estimate=COST,
        name="feedforward_both_ways",
    )(me, *ins)
    made = list(made)
    result = {}
    if last:
        result["outs"], made = made[:ranks], made[ranks:]
        result["n2g"], result["ln2g"], result["ln2b"] = made[:3]
        made = made[3:]
    else:
        result["carried"], made = made[:2], made[2:]
    if first:
        result["w1g"], result["w2g"], result["b1g"], result["mixed_grad"], result["wdg"] = made
    else:
        result["both"], result["b1g"] = made
    return result


def weights_kernel(n1t_ref, dq_ref, dk_ref, dv_ref, out_ref, bg_ref, acc_ref):
    step = pl.program_id(0)

    @pl.when(step == 0)
    def _():
        acc_ref[...] = jnp.zeros_like(acc_ref)
        bg_ref[...] = jnp.zeros_like(bg_ref)

    n1t = n1t_ref[...]
    for which, ref in enumerate((dq_ref, dk_ref, dv_ref)):
        acc_ref[which] += mm(n1t, ref[...])
        bg_ref[which] += fold_rows(ref[...].astype(F32))

    @pl.when(step == pl.num_programs(0) - 1)
    def _():
        out_ref[...] = acc_ref[...].astype(BF)


def weights_backward(index, group, n1t, dq, dk, dv):
    width, length = n1t.shape
    rows = 1024
    return pl.pallas_call(
        weights_kernel,
        grid=(length // rows,),
        in_specs=[across(width, rows)] + [pl.BlockSpec((rows, group), lambda i: (i, index))] * 3,
        out_specs=[fixed((3, width, group)), fixed((3, 8, group))],
        out_shape=[jax.ShapeDtypeStruct((3, width, group), BF), jax.ShapeDtypeStruct((3, 8, group), F32)],
        scratch_shapes=[pltpu.VMEM((3, width, group), F32)],
        compiler_params=pltpu.CompilerParams(vmem_limit_bytes=VMEM),
        cost_estimate=COST,
        name="qkv_weights_backward",
    )(n1t, dq, dk, dv)


def input_kernel(ranks, groups, me_ref, x_ref, gain1_ref, gain2_ref, w_ref, n2g_ref, *refs):
    grads, refs = refs[:3 * groups], refs[3 * groups:]
    outs, refs = refs[:ranks], refs[ranks:]
    lng_ref, lnb_ref, total_ref = refs
    group = grads[0].shape[1]

    @pl.when(pl.program_id(0) == 0)
    def _():
        lng_ref[...] = jnp.zeros_like(lng_ref)
        lnb_ref[...] = jnp.zeros_like(lnb_ref)

    back = None
    for which in range(3):
        for c in range(groups):
            first = (which * groups + c) * group
            term = mm(grads[3 * c + which][...], w_ref[:, first:first + group], NT)
            back = term if back is None else back + term
    xhat, root_inv = norm_rows(x_ref[...].astype(F32))
    lnb_ref[...] += fold_rows(back)
    lng_ref[...] += fold_rows(back * xhat)
    e = back * gain1_ref[...] + n2g_ref[...].astype(F32) * gain2_ref[...]
    total_ref[...] = root_inv * (e - jnp.mean(e, axis=-1, keepdims=True) - xhat * jnp.mean(e * xhat, axis=-1, keepdims=True))
    scatter_pieces(total_ref, me_ref[0], outs)


def input_backward(start, rows, me, ranks, x, gain1, gain2, w, n2g, grads):
    width = x.shape[1]
    group = grads[0].shape[1]
    local = w.shape[1] // 3
    shift = start // T
    piece = lambda cols: pl.BlockSpec((T, cols), lambda i, *_: (i + shift, 0))
    shapes = [((rows, local), F32)] + [((rows, local), BF)] * (ranks - 1)
    return pl.pallas_call(
        functools.partial(input_kernel, ranks, len(grads) // 3),
        grid_spec=pltpu.PrefetchScalarGridSpec(
            num_scalar_prefetch=1,
            grid=(rows // T,),
            in_specs=[piece(width), fixed((1, width)), fixed((1, width)), fixed(w.shape), piece(width)] + [piece(group)] * len(grads),
            out_specs=[tokens(T, s[1]) for s, _ in shapes] + [fixed((8, width))] * 2,
            scratch_shapes=[pltpu.VMEM((T, width), F32)],
        ),
        out_shape=[jax.ShapeDtypeStruct(s, d) for s, d in shapes] + [jax.ShapeDtypeStruct((8, width), F32)] * 2,
        compiler_params=pltpu.CompilerParams(vmem_limit_bytes=VMEM),
        cost_estimate=COST,
        name="input_backward",
    )(me, x, gain1, gain2, w, n2g, *grads)


def rotary_tables(segments):
    length = segments.shape[0]
    places = jnp.arange(length, dtype=jnp.int32)
    first = jnp.concatenate([jnp.ones((1,), dtype=bool), segments[1:] != segments[:-1]])
    starts = lax.cummax(jnp.where(first, places, jnp.zeros_like(places)), axis=0)
    offsets = (places - starts).astype(F32)
    inverse = 10000.0 ** (-jnp.arange(0, ROT, 2).astype(F32) / ROT)
    angles = inverse[:, None] * offsets[None, :]
    return starts, jnp.cos(angles), jnp.sin(angles)


def tie(value, *others):
    return lax.optimization_barrier((value, *others))[0]


def shifted(ranks, distance):
    return [(i, (i + distance) % ranks) for i in range(ranks)]


def send_pieces(pieces):
    ranks = len(pieces)
    came = [lax.ppermute(pieces[d], "tensor", shifted(ranks, d)) for d in range(1, ranks)]
    return sum([c.astype(F32) for c in came], pieces[0]), came


def swap_sum(value, axis, ranks):
    step = 1
    while step < ranks:
        value = value + lax.ppermute(value, axis, [(i, i ^ step) for i in range(ranks)])
        step *= 2
    return value


def pick_kernel(bits_ref, x_ref, out_ref):
    out_ref[...] = x_ref[...]


def merge_kernel(bits_ref, x_ref, came_ref, sent_ref, kept_ref, sum_ref):
    rows = sent_ref.shape[0]
    sum_ref[...] = x_ref[...].astype(F32) + came_ref[...].astype(F32)
    bit = bits_ref[1]
    sent_ref[...] = sum_ref[pl.ds(pl.multiple_of((1 - bit) * rows, rows), rows), :].astype(BF)
    kept_ref[...] = sum_ref[pl.ds(pl.multiple_of(bit * rows, rows), rows), :]


def pick_half(bits, x):
    half, cols = x.shape[0] // 2, x.shape[1]
    quarter = half // 2
    return pl.pallas_call(
        pick_kernel,
        grid_spec=pltpu.PrefetchScalarGridSpec(
            num_scalar_prefetch=1,
            grid=(2,),
            in_specs=[pl.BlockSpec((quarter, cols), lambda i, b: (2 * (1 - b[0]) + i, 0))],
            out_specs=pl.BlockSpec((quarter, cols), lambda i, b: (i, 0)),
        ),
        out_shape=jax.ShapeDtypeStruct((half, cols), BF),
        compiler_params=pltpu.CompilerParams(vmem_limit_bytes=VMEM),
        cost_estimate=COST,
        name="pick_half",
    )(bits, x)


def swap_pair(sent, packs):
    return lax.ppermute(sent, "dp", [(i, i ^ 1) for i in range(packs)])


def merge_halves(bits, x, came):
    half, cols = came.shape
    quarter = half // 2
    return pl.pallas_call(
        merge_kernel,
        grid_spec=pltpu.PrefetchScalarGridSpec(
            num_scalar_prefetch=1,
            grid=(1,),
            in_specs=[pl.BlockSpec((half, cols), lambda i, b: (b[0], 0)), pl.BlockSpec((half, cols), lambda i, b: (0, 0))],
            out_specs=[pl.BlockSpec((quarter, cols), lambda i, b: (0, 0))] * 2,
            scratch_shapes=[pltpu.VMEM((half, cols), F32)],
        ),
        out_shape=[jax.ShapeDtypeStruct((quarter, cols), BF), jax.ShapeDtypeStruct((quarter, cols), F32)],
        compiler_params=pltpu.CompilerParams(vmem_limit_bytes=VMEM),
        cost_estimate=COST,
        name="merge_halves",
    )(bits, x, came)


def cross_sum(sent, kept, packs):
    return kept + lax.ppermute(sent, "dp", [(i, i ^ 2) for i in range(packs)]).astype(F32)


def double(value, packs, step):
    bit = (lax.axis_index("dp") // step) % 2
    other = lax.ppermute(value, "dp", [(i, i ^ step) for i in range(packs)])
    return jnp.where(bit == 0, jnp.concatenate([value, other], axis=0), jnp.concatenate([other, value], axis=0))


def far_shift(packs, far, distance):
    return [(i, ((i // far + distance) * far) % packs + i % far) for i in range(packs)]


def far_sum(value, packs, far):
    count = packs // far
    place = lax.axis_index("dp") // far
    part = value.shape[0] // count
    total = lax.dynamic_slice_in_dim(value, place * part, part, 0)
    for d in range(1, count):
        sent = lax.dynamic_slice_in_dim(value, ((place + d) % count) * part, part, 0).astype(BF)
        total = total + lax.ppermute(sent, "dp", far_shift(packs, far, d)).astype(F32)
    return total


def far_gather(value, packs, far):
    count = packs // far
    place = lax.axis_index("dp") // far
    part = value.shape[0]
    whole = jnp.zeros((count * part,) + value.shape[1:], value.dtype)
    whole = lax.dynamic_update_slice_in_dim(whole, value, place * part, 0)
    for d in range(1, count):
        came = lax.ppermute(value, "dp", far_shift(packs, far, d))
        whole = lax.dynamic_update_slice_in_dim(whole, came, ((place + count - d) % count) * part, 0)
    return whole


def on_device(sizes, inputs, segment_ids, cotangent, ln1_gain, attention_norm_bias, ln2_gain, feedforward_norm_bias, w_qkv, b_qkv, w_dense, b_dense, w_fc1, b_fc1, w_fc2, b_fc2):
    packs, ranks = sizes
    segments = segment_ids[0]
    length, width = inputs.shape
    local = w_qkv.shape[2]
    me = lax.axis_index("tensor").astype(jnp.int32).reshape(1)
    pieces = [cotangent] + [lax.ppermute(cotangent, "tensor", shifted(ranks, ranks - d)) for d in range(1, ranks)]
    starts, cosine, sine = rotary_tables(segments)
    starts = starts.reshape(-1, BQ)
    lowest = starts[:, 0] // BK
    row = lambda v: v.astype(F32).reshape(1, -1)
    qkv_matrix = w_qkv.reshape(width, 3 * local)
    gain1, gain2 = row(ln1_gain), row(ln2_gain)
    shift1, shift2 = row(attention_norm_bias), row(feedforward_norm_bias)
    query, key, value, n1t, n2, n2t = project(inputs, gain1, shift1, gain2, shift2, qkv_matrix, row(b_qkv), cosine, sine)
    mixed, totals = attn_fwd(lowest, starts, query, key, value)
    parts = 2 if w_fc1.shape[1] == 2 * width else 1
    made, carried = [], None
    for part in range(parts):
        made.append(feedforward(part, parts, me, inputs, n2, n2t, w_fc1, row(b_fc1), w_fc2, w_dense, mixed, pieces, carried))
        carried = made[-1].get("carried")
    early = lax.psum((made[0]["w1g"], made[0]["w2g"], made[0]["wdg"]), "dp")
    place = lax.axis_index("dp").astype(jnp.int32)
    bits = jnp.stack([place % 2, (place // 2) % 2])
    late = [m["both"].reshape(2 * width, width) for m in made[1:]]
    picked = [pick_half(bits, v) for v in late]
    swapped = [swap_pair(v, packs) for v in picked]
    own = lax.dynamic_slice_in_dim(inputs, me[0] * local, local, 1).astype(F32)
    total, out_came = send_pieces(made[-1]["outs"])
    outputs = (total + own + b_dense.astype(F32) + b_fc2.astype(F32)).astype(BF)
    mixed_grad = tie(made[0]["mixed_grad"], made[-1]["n2g"], *picked)
    grads = attn_bwd(min(GB * PAIR, local), 0, lowest, starts, query, key, value, mixed, mixed_grad, totals, cosine, sine)
    group = min(2 * PAIR, local)
    groups = local // group
    count = 3 if length % (3 * T) == 0 else 1
    rows = length // count
    weights, biases, input_grad, norms, arrived = [], [], [], [], []

    def chunk(c, normed2_grad):
        got = input_backward(c * rows, rows, me, ranks, inputs, gain1, gain2, qkv_matrix, normed2_grad, grads)
        total, came = send_pieces(got[:ranks])
        arrived.append(came)
        input_grad.append(total + cotangent[c * rows : c * rows + rows].astype(F32))
        norms.append(jnp.stack([jnp.sum(v, axis=0) for v in got[ranks:]]))
        return got[0]

    late = [merge_halves(bits, tie(v, grads[0], *early), s) for v, s in zip(late, swapped)]
    normed2_grad = tie(made[-1]["n2g"], grads[0], *early, *[v[1] for v in late])
    late = [cross_sum(*v, packs) for v in late]
    done = chunk(0, normed2_grad)
    n1t = tie(n1t, done)
    for c in range(groups):
        wg, bg = weights_backward(c, group, n1t, *grads)
        wg = tie(wg, *out_came, *late) if c == 0 else tie(wg, *arrived[0])
        wg = wg.reshape(3 * width, group)
        halves = merge_halves(bits, wg, swap_pair(pick_half(bits, wg), packs))
        n1t = tie(n1t, halves[1])
        if c == 0:
            late = [far_sum(v, packs, 4).astype(BF) for v in late]
        biases.append(jnp.sum(bg, axis=1))
        weights.append(cross_sum(*halves, packs))
    normed2_grad = tie(normed2_grad, halves[1], *arrived[0])
    for c in range(1, count):
        done = chunk(c, normed2_grad)
        if c == 1:
            normed2_grad = tie(normed2_grad, done, *weights, *late)
    late = [far_gather(v, packs, 4) for v in late]
    wg = far_sum(jnp.concatenate(weights, axis=1), packs, 4).astype(BF)
    ready = lax.optimization_barrier((done, wg, norms[-1], *[p for came in arrived[:2] for p in came]))
    wg, norms[-1] = ready[1], ready[2]
    wg = far_gather(wg, packs, 4)
    late = [double(double(v, packs, 2), packs, 1) for v in late]
    input_grad = jnp.concatenate(input_grad, axis=0)
    wg = double(double(wg, packs, 2), packs, 1).astype(F32)
    qkv_weight_grad = wg.reshape(3, width, local).transpose(1, 0, 2)
    norms = jnp.concatenate([sum(norms)] + [jnp.sum(made[-1][n], axis=0, keepdims=True) for n in ("ln2g", "ln2b")], axis=0)
    out_bias = jnp.sum(cotangent.astype(F32), axis=0)
    b1g = [jnp.sum(m["b1g"], axis=0) for m in made]
    bias = jnp.concatenate(biases, axis=1).reshape(-1)
    small = jnp.concatenate([norms.reshape(-1), out_bias, bias] + b1g).reshape(-1, 128)
    small = swap_sum(small, "dp", packs).reshape(-1)
    norms, small = small[: 4 * width].reshape(4, width), small[4 * width :]
    norms = swap_sum(norms, "tensor", ranks)
    dense_bias_grad, small = small[:local], small[local:]
    qkv_bias_grad, fc1_bias_grad = small[: 3 * local].reshape(3, local), small[3 * local :]
    w1g = [v.astype(F32) for v in [early[0]] + [v[:width] for v in late]]
    w2g = [v.astype(F32) for v in [early[1]] + [v[width:] for v in late]]
    return (
        outputs,
        input_grad,
        norms[0],
        norms[1],
        norms[2],
        norms[3],
        qkv_weight_grad,
        qkv_bias_grad,
        early[2].astype(F32),
        dense_bias_grad,
        jnp.concatenate(w1g, axis=1),
        fc1_bias_grad,
        jnp.concatenate(w2g, axis=0),
        dense_bias_grad,
    )


def solution(mesh):
    placed = (
        P("dp", None),
        P("dp", None),
        P("dp", "tensor"),
        P(),
        P(),
        P(),
        P(),
        P(None, None, "tensor"),
        P(None, "tensor"),
        P("tensor", None),
        P("tensor"),
        P(None, "tensor"),
        P("tensor"),
        P("tensor", None),
        P("tensor"),
    )
    sizes = (mesh.shape["dp"], mesh.shape["tensor"])
    return jax.shard_map(
        functools.partial(on_device, sizes),
        mesh=mesh,
        in_specs=placed,
        out_specs=(
            P("dp", "tensor"),
            P("dp", "tensor"),
            P(),
            P(),
            P(),
            P(),
            P(None, None, "tensor"),
            P(None, "tensor"),
            P("tensor", None),
            P("tensor"),
            P(None, "tensor"),
            P("tensor"),
            P("tensor", None),
            P("tensor"),
        ),
        check_vma=False,
    )
```

```python
import functools

import jax
import jax.numpy as jnp
from jax import lax
from jax.experimental import pallas as pl
from jax.experimental.pallas import tpu as pltpu
from jax.sharding import PartitionSpec as P

BQ = 256
BK = 256
PAIR = 128
NEG = -1e30
ROT = 16
NORM_EPS = 1e-05
VMEM = 60 * 1024 * 1024
COST = pl.CostEstimate(flops=1, bytes_accessed=1, transcendentals=0)
GF = 4
GB = 4
AHEAD = 2
BEHIND = 2
AHEADB = 2
BEHINDB = 1
F32 = jnp.float32
BF = jnp.bfloat16
NT = (((1,), (1,)), ((), ()))
NN = (((1,), (0,)), ((), ()))
TN = (((0,), (0,)), ((), ()))

def mm(a, b, dims=NN):
    return lax.dot_general(a, b, dims, preferred_element_type=F32)

def rotary_lanes(cos, sin):
    rest = jnp.ones((64 - ROT, cos.shape[1]), F32)
    none = jnp.zeros((64 - ROT, cos.shape[1]), F32)
    blank = jnp.zeros_like(cos)
    wide = jnp.concatenate([cos, cos, rest] * 2, axis=0)
    low = jnp.concatenate([-sin, blank, none] * 2, axis=0)
    high = jnp.concatenate([blank, sin, none] * 2, axis=0)
    return jnp.transpose(wide), jnp.transpose(low), jnp.transpose(high)


def lane_half(shape):
    return lax.broadcasted_iota(jnp.int32, shape, 1) < 64

def fwd_kernel(lo_ref, start_ref, q_ref, k_ref, v_ref, o_ref, lse_ref, vt_ref):
    length = q_ref.shape[0]
    nq = length // BQ
    nk = length // BK
    groups = q_ref.shape[1] // PAIR
    for i in range(nk):
        vt_ref[i] = jnp.transpose(v_ref[i * BK:(i + 1) * BK, :])
    first = lane_half((BQ, PAIR))

    def q_block(b, _):
        rows = pl.ds(pl.multiple_of(b * BQ, BQ), BQ)
        qs = []
        for g in range(groups):
            q = q_ref[rows, PAIR * g:PAIR * g + PAIR]
            zero = jnp.zeros_like(q)
            qs += [jnp.where(first, q, zero), jnp.where(first, zero, q)]
        starts = start_ref[pl.ds(b, 1), :]
        def step(kb, carry, diagonal):
            keys = pl.ds(pl.multiple_of(kb * BK, BK), BK)
            place = lax.broadcasted_iota(jnp.int32, (BK, BQ), 0)
            allowed = place >= starts - kb * BK
            if diagonal:
                allowed = allowed & (place <= lax.broadcasted_iota(jnp.int32, (BK, BQ), 1))
            heads = range(2 * groups)
            scores, weights, out = {}, {}, []
            def score(h):
                if h in heads:
                    k = k_ref[keys, PAIR * (h // 2):PAIR * (h // 2) + PAIR]
                    scores[h] = mm(k, qs[h], NT)
            def soften(h):
                m, l, acc = carry[h]
                s = jnp.where(allowed, scores[h], NEG)
                m_new = jnp.maximum(m, jnp.max(s, axis=0, keepdims=True))
                p = jnp.exp(s - m_new)
                alpha = jnp.exp(m - m_new)
                weights[h] = (m_new, l * alpha + jnp.sum(p, axis=0, keepdims=True), alpha, p.astype(BF))
            def mix(h):
                m_new, l, alpha, p = weights[h]
                out.append((m_new, l, carry[h][2] * alpha + mm(vt_ref[kb, 64 * h:64 * h + 64, :], p)))
            for h in range(AHEAD):
                score(h)
            for h in heads:
                score(h + AHEAD)
                soften(h)
                if h >= BEHIND:
                    mix(h - BEHIND)
            for h in heads[len(heads) - BEHIND:] if BEHIND else ():
                mix(h)
            return tuple(out)
        init = tuple((jnp.full((1, BQ), NEG, F32), jnp.zeros((1, BQ), F32), jnp.zeros((64, BQ), F32)) for _ in range(2 * groups))
        carry = step(b, init, True)
        carry = lax.fori_loop(lo_ref[b], b, lambda kb, c: step(kb, c, False), carry)
        for h in range(2 * groups):
            lse_ref[h, pl.ds(b, 1), :] = carry[h][0] + jnp.log(carry[h][1])
        ot = jnp.concatenate([c[2] / c[1] for c in carry], axis=0)
        o_ref[rows, :] = jnp.transpose(ot).astype(BF)
        return 0
    lax.fori_loop(0, nq, q_block, 0)

def attn_fwd(lo, starts, q, k, v):
    length, width = q.shape
    nq = length // BQ
    group = min(GF * PAIR, width)
    pairs = width // group
    col = pl.BlockSpec((length, group), lambda p, *_: (0, p))
    return pl.pallas_call(
        fwd_kernel,
        grid_spec=pltpu.PrefetchScalarGridSpec(
            num_scalar_prefetch=1, grid=(pairs,),
            in_specs=[pl.BlockSpec((nq, BQ), lambda p, *_: (0, 0)), col, col, col],
            out_specs=[col, pl.BlockSpec((group // 64, nq, BQ), lambda p, *_: (p, 0, 0))],
            scratch_shapes=[pltpu.VMEM((length // BK, group, BK), BF)],
        ),
        out_shape=[jax.ShapeDtypeStruct((length, width), BF), jax.ShapeDtypeStruct((width // 64, nq, BQ), F32)],
        compiler_params=pltpu.CompilerParams(vmem_limit_bytes=VMEM),
        cost_estimate=COST,
        name="attention_forward",
    )(lo, starts, q, k, v)

def bwd_kernel(lo_ref, start_ref, q_ref, k_ref, v_ref, o_ref, do_ref, lse_ref, cos_ref, sin_ref, dq_ref, dk_ref, dv_ref, kt_ref, dk_acc, dv_acc):
    length = q_ref.shape[0]
    nq = length // BQ
    nk = length // BK
    groups = q_ref.shape[1] // PAIR
    for i in range(nk):
        kt_ref[i] = jnp.transpose(k_ref[i * BK:(i + 1) * BK, :])
    first = lane_half((BQ, PAIR))
    dk_acc[...] = jnp.zeros_like(dk_acc)
    dv_acc[...] = jnp.zeros_like(dv_acc)

    cols = [slice(PAIR * g, PAIR * g + PAIR) for g in range(groups)]

    def q_block(step_index, _):
        b = nq - 1 - step_index
        rows = pl.ds(pl.multiple_of(b * BQ, BQ), BQ)
        starts = start_ref[pl.ds(b, 1), :]
        qs, dos, deltas, lses = [], [], [], []
        for g in range(groups):
            q = q_ref[rows, cols[g]]
            do = do_ref[rows, cols[g]]
            zero = jnp.zeros_like(q)
            qs += [jnp.where(first, q, zero), jnp.where(first, zero, q)]
            dos += [jnp.where(first, do, zero), jnp.where(first, zero, do)]
            prod = jnp.transpose(do.astype(F32) * o_ref[rows, cols[g]].astype(F32))
            deltas += [jnp.sum(prod[:64], axis=0, keepdims=True), jnp.sum(prod[64:], axis=0, keepdims=True)]
            lses += [lse_ref[2 * g, pl.ds(b, 1), :], lse_ref[2 * g + 1, pl.ds(b, 1), :]]
        def step(kb, carry, diagonal):
            keys = pl.ds(pl.multiple_of(kb * BK, BK), BK)
            place = lax.broadcasted_iota(jnp.int32, (BK, BQ), 0)
            allowed = place >= starts - kb * BK
            if diagonal:
                allowed = allowed & (place <= lax.broadcasted_iota(jnp.int32, (BK, BQ), 1))
            out = []
            heads = range(2 * groups)
            raw, soft = {}, {}
            def score(h):
                if h in heads:
                    raw[h] = (mm(k_ref[keys, cols[h // 2]], qs[h], NT), mm(v_ref[keys, cols[h // 2]], dos[h], NT))
            def soften(h):
                s, dp = raw[h]
                p = jnp.exp(jnp.where(allowed, s - lses[h], NEG))
                soft[h] = (p.astype(BF), (p * (dp - deltas[h])).astype(BF))
            def mix(h):
                out.append(carry[h] + mm(kt_ref[kb, 64 * h:64 * h + 64, :], soft[h][1]))
                if h % 2 == 1:
                    g = h // 2
                    dv_acc[keys, cols[g]] += mm(jnp.concatenate([soft[h - 1][0], soft[h][0]], axis=1), jnp.concatenate(dos[2 * g:2 * g + 2], axis=0))
                    dk_acc[keys, cols[g]] += mm(jnp.concatenate([soft[h - 1][1], soft[h][1]], axis=1), jnp.concatenate(qs[2 * g:2 * g + 2], axis=0))
            for h in range(AHEADB):
                score(h)
            for h in heads:
                score(h + AHEADB)
                soften(h)
                if h >= BEHINDB:
                    mix(h - BEHINDB)
            for h in heads[len(heads) - BEHINDB:] if BEHINDB else ():
                mix(h)
            return tuple(out)
        carry = tuple(jnp.zeros((64, BQ), F32) for _ in range(2 * groups))
        carry = lax.fori_loop(lo_ref[b], b, lambda kb, c: step(kb, c, False), carry)
        carry = step(b, carry, True)
        cos, sin = cos_ref[:, rows], sin_ref[:, rows]
        wide, low, high = rotary_lanes(cos, sin)
        for g in range(groups):
            turned = []
            for w in carry[2 * g:2 * g + 2]:
                turned += [w[:8] * cos + w[8:16] * sin, w[8:16] * cos - w[:8] * sin, w[16:]]
            dq_ref[rows, cols[g]] = (jnp.transpose(jnp.concatenate(turned, axis=0)) * 0.125).astype(BF)
            dk = dk_acc[rows, cols[g]]
            dk = dk * wide - pltpu.roll(dk, PAIR - 8, 1) * low - pltpu.roll(dk, 8, 1) * high
            dk_ref[rows, cols[g]] = dk.astype(BF)
            dv_ref[rows, cols[g]] = dv_acc[rows, cols[g]].astype(BF)
        return 0
    lax.fori_loop(0, nq, q_block, 0)

def attn_bwd(group, index, lo, starts, q, k, v, o, do, lse, cos, sin):
    length = q.shape[0]
    nq = length // BQ
    col = pl.BlockSpec((length, group), lambda p, *_: (0, index))
    own = pl.BlockSpec((length, group), lambda p, *_: (0, 0))
    whole = pl.BlockSpec((ROT // 2, length), lambda p, *_: (0, 0))
    return pl.pallas_call(
        bwd_kernel,
        grid_spec=pltpu.PrefetchScalarGridSpec(
            num_scalar_prefetch=1, grid=(1,),
            in_specs=[pl.BlockSpec((nq, BQ), lambda p, *_: (0, 0)), col, col, col, col, col,
                      pl.BlockSpec((group // 64, nq, BQ), lambda p, *_: (index, 0, 0)), whole, whole],
            out_specs=[own, own, own],
            scratch_shapes=[pltpu.VMEM((length // BK, group, BK), BF), pltpu.VMEM((length, group), F32), pltpu.VMEM((length, group), F32)],
        ),
        out_shape=[jax.ShapeDtypeStruct((length, group), BF)] * 3,
        compiler_params=pltpu.CompilerParams(vmem_limit_bytes=VMEM),
        cost_estimate=COST,
        name="attention_backward",
    )(lo, starts, q, k, v, o, do, lse, cos, sin)

T = 512
TT = 512


def norm_rows(x, eps=NORM_EPS):
    centred = x - jnp.mean(x, axis=-1, keepdims=True)
    root_inv = lax.rsqrt(jnp.mean(centred * centred, axis=-1, keepdims=True) + eps)
    return centred * root_inv, root_inv


def fold_rows(v):
    return jnp.sum(v.reshape(v.shape[0] // 8, 8, v.shape[1]), axis=0)


def project_kernel(x_ref, gain_ref, shift_ref, gain2_ref, shift2_ref, w_ref, b_ref, cos_ref, sin_ref, q_ref, k_ref, v_ref, n1t_ref, n2_ref, n2t_ref):
    local = q_ref.shape[1]
    xhat, _ = norm_rows(x_ref[...].astype(F32))
    normed = (xhat * gain_ref[...] + shift_ref[...]).astype(BF)
    n1t_ref[...] = jnp.transpose(normed)
    normed2 = (xhat * gain2_ref[...] + shift2_ref[...]).astype(BF)
    n2_ref[...] = normed2
    n2t_ref[...] = jnp.transpose(normed2)
    wide, low, high = rotary_lanes(cos_ref[...], sin_ref[...])
    for which, out in enumerate((q_ref, k_ref, v_ref)):
        span = slice(which * local, which * local + local)
        y = mm(normed, w_ref[:, span]) + b_ref[:, span]
        if which == 2:
            out[...] = y.astype(BF)
            continue
        for c in range(local // PAIR):
            cols = slice(c * PAIR, c * PAIR + PAIR)
            u = y[:, cols]
            u = u * wide + pltpu.roll(u, PAIR - 8, 1) * low + pltpu.roll(u, 8, 1) * high
            out[:, cols] = (u * 0.125 if which == 0 else u).astype(BF)


def fixed(shape):
    return pl.BlockSpec(shape, lambda i, *_: (0,) * len(shape), pipeline_mode=pl.Buffered(1))


def tokens(rows, cols):
    return pl.BlockSpec((rows, cols), lambda i, *_: (i, 0))


def across(rows, cols):
    return pl.BlockSpec((rows, cols), lambda i, *_: (0, i))


def project(x, gain, shift, gain2, shift2, w, b, cos, sin):
    length, width = x.shape
    local = w.shape[1] // 3
    return pl.pallas_call(
        project_kernel,
        grid=(length // T,),
        in_specs=[tokens(T, width)] + [fixed((1, width))] * 4 + [fixed(w.shape), fixed(b.shape)] + [across(ROT // 2, T)] * 2,
        out_specs=[tokens(T, local)] * 3 + [across(width, T), tokens(T, width), across(width, T)],
        out_shape=[jax.ShapeDtypeStruct(s, BF) for s in ((length, local),) * 3 + ((width, length), (length, width), (width, length))],
        compiler_params=pltpu.CompilerParams(vmem_limit_bytes=VMEM),
        cost_estimate=COST,
        name="project_qkv",
    )(x, gain, shift, gain2, shift2, w, b, cos, sin)


def scatter_pieces(total, me, outs):
    ranks, local = len(outs), outs[0].shape[1]
    for d in range(ranks):
        target = lax.rem(me + d, ranks)
        cols = pl.ds(pl.multiple_of(target * local, 128), local)
        outs[d][...] = total[:, cols].astype(outs[d].dtype)


def feedforward_kernel(ranks, part, parts, me_ref, n2_ref, n2t_ref, w1_ref, b1_ref, w2_ref, *refs):
    first, last = part == 0, part == parts - 1
    pieces, refs = refs[:ranks], refs[ranks:]
    if first:
        (wd_ref, mixed_ref), refs = refs[:2], refs[2:]
    else:
        (total_in, back_in), refs = refs[:2], refs[2:]
    if last:
        (x_ref,), refs = refs[:1], refs[1:]
        outs, refs = refs[:ranks], refs[ranks:]
        (n2g_ref, lng_ref, lnb_ref), refs = refs[:3], refs[3:]
        sums = [lng_ref, lnb_ref]
    else:
        (total_out, back_out), refs = refs[:2], refs[2:]
        sums = []
    if first:
        (w1_out, w2_out), refs = refs[:2], refs[2:]
    else:
        w1_out, w2_out, refs = refs[0].at[0], refs[0].at[1], refs[1:]
    (b1g_ref,), refs = refs[:1], refs[1:]
    if first:
        (mixed_grad_ref, wd_out), refs = refs[:2], refs[2:]
        (wdg_ref,), refs = refs[:1], refs[1:]
        sums.append(wdg_ref)
    w1g_ref, w2g_ref, g_ref, total_ref, back_ref = refs
    step = pl.program_id(0)
    me = me_ref[0]
    local = pieces[0].shape[1]
    hidden_units = w1_ref.shape[1]
    chunk = min(512, hidden_units)
    chunks = hidden_units // chunk

    @pl.when(step == 0)
    def _():
        for ref in [w1g_ref, w2g_ref, b1g_ref] + sums:
            ref[...] = jnp.zeros_like(ref)

    for d in range(ranks):
        source = lax.rem(me + d, ranks)
        g_ref[:, pl.ds(pl.multiple_of(source * local, 128), local)] = pieces[d][...]
    normed = n2_ref[...]
    g = g_ref[...]
    raw, soft = {}, {}

    def expand(c):
        if c < chunks:
            cols = slice(c * chunk, c * chunk + chunk)
            raw[c] = (mm(normed, w1_ref[:, cols]) + b1_ref[:, cols], mm(g, w2_ref[cols, :], NT))

    def bend(c):
        cols = slice(c * chunk, c * chunk + chunk)
        hidden, active_grad = raw[c]
        cumulative = 0.5 * (1.0 + lax.erf(hidden * 0.7071067811865476))
        density = jnp.exp(-0.5 * hidden * hidden) * 0.3989422804014327
        active = (hidden * cumulative).astype(BF)
        hidden_grad = (active_grad * (cumulative + hidden * density)).astype(BF)
        b1g_ref[:, cols] += fold_rows(hidden_grad.astype(F32))
        soft[c] = (active, hidden_grad)

    def contract(c):
        cols = slice(c * chunk, c * chunk + chunk)
        active, hidden_grad = soft[c]
        feed = mm(active, w2_ref[cols, :])
        back = mm(hidden_grad, w1_ref[:, cols], NT)
        if c == 0 and first:
            total_ref[...] = feed
            back_ref[...] = back
        elif c == 0:
            total_ref[...] = total_in[...] + feed
            back_ref[...] = back_in[...] + back
        else:
            total_ref[...] += feed
            back_ref[...] += back
        w2g_ref[cols, :] += mm(active, g, TN)
        w1g_ref[:, cols] += mm(n2t_ref[...], hidden_grad)

    expand(0)
    for c in range(chunks):
        expand(c + 1)
        bend(c)
        if c >= 1:
            contract(c - 1)
    if first:
        mixed = mixed_ref[...]
        mixed_grad_ref[...] = mm(g, wd_ref[...], NT).astype(BF)
        wdg_ref[...] += mm(mixed, g, TN)
    contract(chunks - 1)
    if first:
        total_ref[...] += mm(mixed, wd_ref[...])
    if last:
        xhat, _ = norm_rows(x_ref[...].astype(F32))
        back = back_ref[...]
        n2g_ref[...] = back.astype(BF)
        lnb_ref[...] += fold_rows(back)
        lng_ref[...] += fold_rows(back * xhat)
        scatter_pieces(total_ref, me, outs)
    else:
        total_out[...] = total_ref[...]
        back_out[...] = back_ref[...]

    @pl.when(step == pl.num_programs(0) - 1)
    def _():
        w1_out[...] = w1g_ref[...].astype(BF)
        w2_out[...] = w2g_ref[...].astype(BF)
        if first:
            wd_out[...] = wdg_ref[...].astype(BF)


def feedforward(part, parts, me, x, n2, n2t, w1, b1, w2, wd, mixed, pieces, carried):
    length, width = x.shape
    local, ranks = pieces[0].shape[1], len(pieces)
    units = w1.shape[1] // parts
    first, last = part == 0, part == parts - 1
    lone = dict(pipeline_mode=pl.Buffered(1))
    ins = [n2, n2t, w1, b1, w2, *pieces]
    specs = [
        tokens(TT, width),
        across(width, TT),
        pl.BlockSpec((width, units), lambda i, *_: (0, part), **lone),
        pl.BlockSpec((1, units), lambda i, *_: (0, part), **lone),
        pl.BlockSpec((units, width), lambda i, *_: (part, 0), **lone),
    ] + [tokens(TT, local)] * ranks
    if first:
        ins += [wd, mixed]
        specs += [fixed(wd.shape), tokens(TT, local)]
    else:
        ins += list(carried)
        specs += [tokens(TT, width)] * 2
    outs = []
    if last:
        ins.append(x)
        specs.append(tokens(TT, width))
        outs += [(tokens(TT, local), (length, local), F32)] + [(tokens(TT, local), (length, local), BF)] * (ranks - 1)
        outs += [(tokens(TT, width), (length, width), BF)] + [(fixed((8, width)), (8, width), F32)] * 2
    else:
        outs += [(tokens(TT, width), (length, width), F32)] * 2
    if first:
        outs += [(fixed((width, units)), (width, units), BF), (fixed((units, width)), (units, width), BF)]
    else:
        outs.append((fixed((2, width, units)), (2, width, units), BF))
    outs.append((fixed((8, units)), (8, units), F32))
    scratch = []
    if first:
        outs += [(tokens(TT, local), (length, local), BF), (fixed((local, width)), (local, width), BF)]
        scratch.append(pltpu.VMEM((local, width), F32))
    scratch += [pltpu.VMEM((width, units), F32), pltpu.VMEM((units, width), F32), pltpu.VMEM((TT, width), BF), pltpu.VMEM((TT, width), F32), pltpu.VMEM((TT, width), F32)]
    made = pl.pallas_call(
        functools.partial(feedforward_kernel, ranks, part, parts),
        grid_spec=pltpu.PrefetchScalarGridSpec(
            num_scalar_prefetch=1,
            grid=(length // TT,),
            in_specs=specs,
            out_specs=[o[0] for o in outs],
            scratch_shapes=scratch,
        ),
        out_shape=[jax.ShapeDtypeStruct(o[1], o[2]) for o in outs],
        compiler_params=pltpu.CompilerParams(vmem_limit_bytes=VMEM),
        cost_estimate=COST,
        name="feedforward_both_ways",
    )(me, *ins)
    made = list(made)
    result = {}
    if last:
        result["outs"], made = made[:ranks], made[ranks:]
        result["n2g"], result["ln2g"], result["ln2b"] = made[:3]
        made = made[3:]
    else:
        result["carried"], made = made[:2], made[2:]
    if first:
        result["w1g"], result["w2g"], result["b1g"], result["mixed_grad"], result["wdg"] = made
    else:
        result["both"], result["b1g"] = made
    return result


def weights_kernel(n1t_ref, dq_ref, dk_ref, dv_ref, out_ref, bg_ref, acc_ref):
    step = pl.program_id(0)

    @pl.when(step == 0)
    def _():
        acc_ref[...] = jnp.zeros_like(acc_ref)
        bg_ref[...] = jnp.zeros_like(bg_ref)

    n1t = n1t_ref[...]
    for which, ref in enumerate((dq_ref, dk_ref, dv_ref)):
        acc_ref[which] += mm(n1t, ref[...])
        bg_ref[which] += fold_rows(ref[...].astype(F32))

    @pl.when(step == pl.num_programs(0) - 1)
    def _():
        out_ref[...] = acc_ref[...].astype(BF)


def weights_backward(index, group, n1t, dq, dk, dv):
    width, length = n1t.shape
    rows = 1024
    return pl.pallas_call(
        weights_kernel,
        grid=(length // rows,),
        in_specs=[across(width, rows)] + [pl.BlockSpec((rows, group), lambda i: (i, index))] * 3,
        out_specs=[fixed((3, width, group)), fixed((3, 8, group))],
        out_shape=[jax.ShapeDtypeStruct((3, width, group), BF), jax.ShapeDtypeStruct((3, 8, group), F32)],
        scratch_shapes=[pltpu.VMEM((3, width, group), F32)],
        compiler_params=pltpu.CompilerParams(vmem_limit_bytes=VMEM),
        cost_estimate=COST,
        name="qkv_weights_backward",
    )(n1t, dq, dk, dv)


def input_kernel(ranks, groups, me_ref, x_ref, gain1_ref, gain2_ref, w_ref, n2g_ref, *refs):
    grads, refs = refs[:3 * groups], refs[3 * groups:]
    outs, refs = refs[:ranks], refs[ranks:]
    lng_ref, lnb_ref, total_ref = refs
    group = grads[0].shape[1]

    @pl.when(pl.program_id(0) == 0)
    def _():
        lng_ref[...] = jnp.zeros_like(lng_ref)
        lnb_ref[...] = jnp.zeros_like(lnb_ref)

    back = None
    for which in range(3):
        for c in range(groups):
            first = (which * groups + c) * group
            term = mm(grads[3 * c + which][...], w_ref[:, first:first + group], NT)
            back = term if back is None else back + term
    xhat, root_inv = norm_rows(x_ref[...].astype(F32))
    lnb_ref[...] += fold_rows(back)
    lng_ref[...] += fold_rows(back * xhat)
    e = back * gain1_ref[...] + n2g_ref[...].astype(F32) * gain2_ref[...]
    total_ref[...] = root_inv * (e - jnp.mean(e, axis=-1, keepdims=True) - xhat * jnp.mean(e * xhat, axis=-1, keepdims=True))
    scatter_pieces(total_ref, me_ref[0], outs)


def input_backward(start, rows, me, ranks, x, gain1, gain2, w, n2g, grads):
    width = x.shape[1]
    group = grads[0].shape[1]
    local = w.shape[1] // 3
    shift = start // T
    piece = lambda cols: pl.BlockSpec((T, cols), lambda i, *_: (i + shift, 0))
    shapes = [((rows, local), F32)] + [((rows, local), BF)] * (ranks - 1)
    return pl.pallas_call(
        functools.partial(input_kernel, ranks, len(grads) // 3),
        grid_spec=pltpu.PrefetchScalarGridSpec(
            num_scalar_prefetch=1,
            grid=(rows // T,),
            in_specs=[piece(width), fixed((1, width)), fixed((1, width)), fixed(w.shape), piece(width)] + [piece(group)] * len(grads),
            out_specs=[tokens(T, s[1]) for s, _ in shapes] + [fixed((8, width))] * 2,
            scratch_shapes=[pltpu.VMEM((T, width), F32)],
        ),
        out_shape=[jax.ShapeDtypeStruct(s, d) for s, d in shapes] + [jax.ShapeDtypeStruct((8, width), F32)] * 2,
        compiler_params=pltpu.CompilerParams(vmem_limit_bytes=VMEM),
        cost_estimate=COST,
        name="input_backward",
    )(me, x, gain1, gain2, w, n2g, *grads)


def rotary_tables(segments):
    length = segments.shape[0]
    places = jnp.arange(length, dtype=jnp.int32)
    first = jnp.concatenate([jnp.ones((1,), dtype=bool), segments[1:] != segments[:-1]])
    starts = lax.cummax(jnp.where(first, places, jnp.zeros_like(places)), axis=0)
    offsets = (places - starts).astype(F32)
    inverse = 10000.0 ** (-jnp.arange(0, ROT, 2).astype(F32) / ROT)
    angles = inverse[:, None] * offsets[None, :]
    return starts, jnp.cos(angles), jnp.sin(angles)


def tie(value, *others):
    return lax.optimization_barrier((value, *others))[0]


def shifted(ranks, distance):
    return [(i, (i + distance) % ranks) for i in range(ranks)]


def send_pieces(pieces):
    ranks = len(pieces)
    came = [lax.ppermute(pieces[d], "tensor", shifted(ranks, d)) for d in range(1, ranks)]
    return sum([c.astype(F32) for c in came], pieces[0]), came


def swap_sum(value, axis, ranks):
    step = 1
    while step < ranks:
        value = value + lax.ppermute(value, axis, [(i, i ^ step) for i in range(ranks)])
        step *= 2
    return value


def pick_kernel(bits_ref, x_ref, out_ref):
    out_ref[...] = x_ref[...]


def merge_kernel(bits_ref, x_ref, came_ref, sent_ref, kept_ref, sum_ref):
    rows = sent_ref.shape[0]
    sum_ref[...] = x_ref[...].astype(F32) + came_ref[...].astype(F32)
    bit = bits_ref[1]
    sent_ref[...] = sum_ref[pl.ds(pl.multiple_of((1 - bit) * rows, rows), rows), :].astype(BF)
    kept_ref[...] = sum_ref[pl.ds(pl.multiple_of(bit * rows, rows), rows), :]


def pick_half(bits, x):
    half, cols = x.shape[0] // 2, x.shape[1]
    quarter = half // 2
    return pl.pallas_call(
        pick_kernel,
        grid_spec=pltpu.PrefetchScalarGridSpec(
            num_scalar_prefetch=1,
            grid=(2,),
            in_specs=[pl.BlockSpec((quarter, cols), lambda i, b: (2 * (1 - b[0]) + i, 0))],
            out_specs=pl.BlockSpec((quarter, cols), lambda i, b: (i, 0)),
        ),
        out_shape=jax.ShapeDtypeStruct((half, cols), BF),
        compiler_params=pltpu.CompilerParams(vmem_limit_bytes=VMEM),
        cost_estimate=COST,
        name="pick_half",
    )(bits, x)


def swap_pair(sent, packs):
    return lax.ppermute(sent, "dp", [(i, i ^ 1) for i in range(packs)])


def merge_halves(bits, x, came):
    half, cols = came.shape
    quarter = half // 2
    return pl.pallas_call(
        merge_kernel,
        grid_spec=pltpu.PrefetchScalarGridSpec(
            num_scalar_prefetch=1,
            grid=(1,),
            in_specs=[pl.BlockSpec((half, cols), lambda i, b: (b[0], 0)), pl.BlockSpec((half, cols), lambda i, b: (0, 0))],
            out_specs=[pl.BlockSpec((quarter, cols), lambda i, b: (0, 0))] * 2,
            scratch_shapes=[pltpu.VMEM((half, cols), F32)],
        ),
        out_shape=[jax.ShapeDtypeStruct((quarter, cols), BF), jax.ShapeDtypeStruct((quarter, cols), F32)],
        compiler_params=pltpu.CompilerParams(vmem_limit_bytes=VMEM),
        cost_estimate=COST,
        name="merge_halves",
    )(bits, x, came)


def cross_sum(sent, kept, packs):
    return kept + lax.ppermute(sent, "dp", [(i, i ^ 2) for i in range(packs)]).astype(F32)


def double(value, packs, step):
    bit = (lax.axis_index("dp") // step) % 2
    other = lax.ppermute(value, "dp", [(i, i ^ step) for i in range(packs)])
    return jnp.where(bit == 0, jnp.concatenate([value, other], axis=0), jnp.concatenate([other, value], axis=0))


def far_shift(packs, far, distance):
    return [(i, ((i // far + distance) * far) % packs + i % far) for i in range(packs)]


def far_sum(value, packs, far):
    count = packs // far
    place = lax.axis_index("dp") // far
    part = value.shape[0] // count
    total = lax.dynamic_slice_in_dim(value, place * part, part, 0)
    for d in range(1, count):
        sent = lax.dynamic_slice_in_dim(value, ((place + d) % count) * part, part, 0).astype(BF)
        total = total + lax.ppermute(sent, "dp", far_shift(packs, far, d)).astype(F32)
    return total


def far_gather(value, packs, far):
    count = packs // far
    place = lax.axis_index("dp") // far
    part = value.shape[0]
    whole = jnp.zeros((count * part,) + value.shape[1:], value.dtype)
    whole = lax.dynamic_update_slice_in_dim(whole, value, place * part, 0)
    for d in range(1, count):
        came = lax.ppermute(value, "dp", far_shift(packs, far, d))
        whole = lax.dynamic_update_slice_in_dim(whole, came, ((place + count - d) % count) * part, 0)
    return whole


def on_device(sizes, inputs, segment_ids, cotangent, ln1_gain, attention_norm_bias, ln2_gain, feedforward_norm_bias, w_qkv, b_qkv, w_dense, b_dense, w_fc1, b_fc1, w_fc2, b_fc2):
    packs, ranks = sizes
    segments = segment_ids[0]
    length, width = inputs.shape
    local = w_qkv.shape[2]
    me = lax.axis_index("tensor").astype(jnp.int32).reshape(1)
    pieces = [cotangent] + [lax.ppermute(cotangent, "tensor", shifted(ranks, ranks - d)) for d in range(1, ranks)]
    starts, cosine, sine = rotary_tables(segments)
    starts = starts.reshape(-1, BQ)
    lowest = starts[:, 0] // BK
    row = lambda v: v.astype(F32).reshape(1, -1)
    qkv_matrix = w_qkv.reshape(width, 3 * local)
    gain1, gain2 = row(ln1_gain), row(ln2_gain)
    shift1, shift2 = row(attention_norm_bias), row(feedforward_norm_bias)
    query, key, value, n1t, n2, n2t = project(inputs, gain1, shift1, gain2, shift2, qkv_matrix, row(b_qkv), cosine, sine)
    mixed, totals = attn_fwd(lowest, starts, query, key, value)
    parts = 2 if w_fc1.shape[1] == 2 * width else 1
    made, carried = [], None
    for part in range(parts):
        made.append(feedforward(part, parts, me, inputs, n2, n2t, w_fc1, row(b_fc1), w_fc2, w_dense, mixed, pieces, carried))
        carried = made[-1].get("carried")
    place = lax.axis_index("dp").astype(jnp.int32)
    bits = jnp.stack([place % 2, (place // 2) % 2])
    both = [m["both"].reshape(2 * width, width) for m in made[1:]]
    early = lax.psum((made[0]["w1g"], made[0]["w2g"], made[0]["wdg"], *both), "dp")
    late = early[3:]
    own = lax.dynamic_slice_in_dim(inputs, me[0] * local, local, 1).astype(F32)
    total, out_came = send_pieces(made[-1]["outs"])
    outputs = (total + own + b_dense.astype(F32) + b_fc2.astype(F32)).astype(BF)
    mixed_grad = tie(made[0]["mixed_grad"], made[-1]["n2g"])
    grads = attn_bwd(min(GB * PAIR, local), 0, lowest, starts, query, key, value, mixed, mixed_grad, totals, cosine, sine)
    group = min(2 * PAIR, local)
    groups = local // group
    count = 3 if length % (3 * T) == 0 else 1
    rows = length // count
    weights, biases, input_grad, norms, arrived = [], [], [], [], []

    def chunk(c, normed2_grad):
        got = input_backward(c * rows, rows, me, ranks, inputs, gain1, gain2, qkv_matrix, normed2_grad, grads)
        total, came = send_pieces(got[:ranks])
        arrived.append(came)
        input_grad.append(total + cotangent[c * rows : c * rows + rows].astype(F32))
        norms.append(jnp.stack([jnp.sum(v, axis=0) for v in got[ranks:]]))
        return got[0]

    normed2_grad = tie(made[-1]["n2g"], grads[0])
    done = chunk(0, normed2_grad)
    n1t = tie(n1t, done)
    for c in range(groups):
        wg, bg = weights_backward(c, group, n1t, *grads)
        wg = tie(wg, *out_came) if c == 0 else tie(wg, *arrived[0])
        wg = wg.reshape(3 * width, group)
        halves = merge_halves(bits, wg, swap_pair(pick_half(bits, wg), packs))
        n1t = tie(n1t, halves[1])
        biases.append(jnp.sum(bg, axis=1))
        weights.append(cross_sum(*halves, packs))
    normed2_grad = tie(normed2_grad, halves[1], *arrived[0])
    for c in range(1, count):
        done = chunk(c, normed2_grad)
        if c == 1:
            normed2_grad = tie(normed2_grad, done, *weights)
    wg = far_sum(jnp.concatenate(weights, axis=1), packs, 4).astype(BF)
    ready = lax.optimization_barrier((done, wg, norms[-1], *[p for came in arrived[:2] for p in came]))
    wg, norms[-1] = ready[1], ready[2]
    wg = far_gather(wg, packs, 4)
    norms[-1] = tie(norms[-1], *[p for came in arrived for p in came])
    input_grad = jnp.concatenate(input_grad, axis=0)
    wg = double(double(wg, packs, 2), packs, 1).astype(F32)
    qkv_weight_grad = wg.reshape(3, width, local).transpose(1, 0, 2)
    norms = jnp.concatenate([sum(norms)] + [jnp.sum(made[-1][n], axis=0, keepdims=True) for n in ("ln2g", "ln2b")], axis=0)
    out_bias = jnp.sum(cotangent.astype(F32), axis=0)
    b1g = [jnp.sum(m["b1g"], axis=0) for m in made]
    bias = jnp.concatenate(biases, axis=1).reshape(-1)
    small = jnp.concatenate([norms.reshape(-1), out_bias, bias] + b1g).reshape(-1, 128)
    small = swap_sum(small, "dp", packs).reshape(-1)
    norms, small = small[: 4 * width].reshape(4, width), small[4 * width :]
    norms = swap_sum(norms, "tensor", ranks)
    dense_bias_grad, small = small[:local], small[local:]
    qkv_bias_grad, fc1_bias_grad = small[: 3 * local].reshape(3, local), small[3 * local :]
    w1g = [v.astype(F32) for v in [early[0]] + [v[:width] for v in late]]
    w2g = [v.astype(F32) for v in [early[1]] + [v[width:] for v in late]]
    return (
        outputs,
        input_grad,
        norms[0],
        norms[1],
        norms[2],
        norms[3],
        qkv_weight_grad,
        qkv_bias_grad,
        early[2].astype(F32),
        dense_bias_grad,
        jnp.concatenate(w1g, axis=1),
        fc1_bias_grad,
        jnp.concatenate(w2g, axis=0),
        dense_bias_grad,
    )


def solution(mesh):
    placed = (
        P("dp", None),
        P("dp", None),
        P("dp", "tensor"),
        P(),
        P(),
        P(),
        P(),
        P(None, None, "tensor"),
        P(None, "tensor"),
        P("tensor", None),
        P("tensor"),
        P(None, "tensor"),
        P("tensor"),
        P("tensor", None),
        P("tensor"),
    )
    sizes = (mesh.shape["dp"], mesh.shape["tensor"])
    return jax.shard_map(
        functools.partial(on_device, sizes),
        mesh=mesh,
        in_specs=placed,
        out_specs=(
            P("dp", "tensor"),
            P("dp", "tensor"),
            P(),
            P(),
            P(),
            P(),
            P(None, None, "tensor"),
            P(None, "tensor"),
            P("tensor", None),
            P("tensor"),
            P(None, "tensor"),
            P("tensor"),
            P("tensor", None),
            P("tensor"),
        ),
        check_vma=False,
    )
```
